256 devices in a mesh: cls: 32 (over x, z), img: 8 (over y, core).
Axes of the slice: x: 4, y: 4, z: 8, core: 2. Of those that a mesh axis runs over, the one named last changes fastest.
Arguments:
- images: bfloat16 [4096, 9216], P(('cls', 'img')), may hold values from -9 to 9
- ctf: bfloat16 [4096, 4608], P(('cls', 'img')), may hold values from -1 to 1
- classes: int32 [4096, 4], P(('cls', 'img')), may hold values from 0 to 223, as said below
- class_place: int32 [224], replicated, may hold values from 0 to 223, as said below
- references: bfloat16 [224, 9216], P('cls'), may hold values from -3 to 3
- sigma2: float32 [64], replicated, may hold values from 0.05 to 4, as said below
Outputs:
- new_references: float32 [224, 9216], P('cls', 'img')
The draws below stay inside these ranges and needn't reach their ends.
Inputs may be any that keep to these rules, and one draw needn't show every extreme that they name: Each particle names 4 different classes whose table rows class_place[k] lie in 4 different groups of 7 consecutive table rows. Among the 16 particles of one device (aligned blocks of 16 rows) at most 8 list entries fall in one group, and in every block some group receives exactly 8. A permutation: class k is held in table row class_place[k]. `sigma2`: positive noise powers.
All inputs are finite; a program needn't handle non-finite values.
Results may differ from the reference program's by a relative error of at most 0.0018.
Values may be sent and summed in bfloat16 or wider, within the bound.
No kernel may reach another device: no remote copies, remote signals or barrier semaphores. Data moves between devices by JAX's collectives and lax.ppermute only.
A program may use at most 128 MiB of HBM per device.

```python
import math
import jax
import jax.numpy as jnp
from jax import lax

S = 64
NA = 72
TOP = 4
K_DEV = 7
P_DEV = 16
CAP = 8
K = 224
NP = 4096


def routing_tables(key):
    owners = K // K_DEV
    blocks = NP // P_DEV
    groups = blocks // owners
    pick_count = TOP * P_DEV
    placement = jax.random.permutation(jax.random.fold_in(key, 7), K).astype(jnp.int32)
    inverse = jnp.zeros((K,), jnp.int32).at[placement].set(jnp.arange(K, dtype=jnp.int32))
    hot_group = jax.random.randint(jax.random.fold_in(key, 8), (groups,), 0, owners)
    hot_block = hot_group[jnp.arange(blocks) % groups]
    block_keys = jax.random.split(jax.random.fold_in(key, 9), blocks)
    remaining = pick_count - CAP
    even_load = remaining // (owners - 1)
    extra_load = remaining % (owners - 1)
    pair_count = max((owners - 1) // 2, 1)

    def one_block(block_key, hot_owner):
        key_rank, key_move, key_order, key_offset, key_rows = jax.random.split(block_key, 5)
        ordering = jax.random.permutation(key_rank, owners)
        ranking = jnp.zeros((owners,), jnp.int32).at[ordering].set(jnp.arange(owners, dtype=jnp.int32))
        other_rank = ranking - (ranking > ranking[hot_owner]).astype(jnp.int32)
        loads = even_load + (other_rank < extra_load).astype(jnp.int32)
        pair_index = jnp.arange(pair_count, dtype=jnp.int32)
        low_load = even_load + (2 * pair_index < extra_load).astype(jnp.int32)
        high_load = even_load + (2 * pair_index + 1 < extra_load).astype(jnp.int32)
        move_limit = jnp.maximum(jnp.minimum(low_load, CAP - high_load), 0)
        shifted_by = jax.random.randint(key_move, (pair_count,), 0, move_limit + 1)
        paired = other_rank < 2 * ((owners - 1) // 2)
        partner = jnp.minimum(other_rank // 2, pair_count - 1)
        change = jnp.where(other_rank % 2 == 0, -shifted_by[partner], shifted_by[partner])
        loads = jnp.where(paired, loads + change, loads)
        loads = jnp.where(jnp.arange(owners) == hot_owner, CAP, loads).astype(jnp.int32)
        sequence = jax.random.permutation(key_order, owners)
        ordered = loads[sequence]
        run_end = jnp.cumsum(ordered)
        starts = run_end - ordered
        pick_slot = jnp.arange(pick_count, dtype=jnp.int32)
        position = jnp.sum((pick_slot[:, None] >= run_end[None, :]).astype(jnp.int32), axis=1)
        owner_id = sequence[position]
        within = pick_slot - starts[position]
        offset = jax.random.randint(key_offset, (owners,), 0, K_DEV)
        table_row = owner_id * K_DEV + (offset[owner_id] + within) % K_DEV
        chosen = inverse[table_row].reshape(TOP, P_DEV).T
        return chosen[jax.random.permutation(key_rows, P_DEV)]
    class_lists = jax.vmap(one_block)(block_keys, hot_block)
    return (placement, class_lists.reshape(NP, TOP).astype(jnp.int32))


def bright_setup(key):
    bright_count = max(1, K // 32)
    bright_rows = jax.random.permutation(jax.random.fold_in(key, 21), K)[:bright_count]
    is_bright = jnp.zeros((K,), jnp.bool_).at[bright_rows].set(True)
    strength = jax.random.uniform(jax.random.fold_in(key, 22), (K,), jnp.float32, 1.5, 3.0)
    amplitude = jnp.where(is_bright, jnp.sqrt(536.0 * strength / (S * NA)), 0.05)
    return (is_bright, amplitude)


def draw_classes(key, part):
    return routing_tables(key)[1]


def draw_class_place(key, part):
    return routing_tables(key)[0]


def draw_sigma2(key, part):
    spread = jax.random.uniform(key, (S,), jnp.float32, math.log(0.5), math.log(4.0))
    noise_power = jnp.exp(spread)
    return noise_power.astype(jnp.float32)


def draw_references(key, part):
    is_bright, amplitude = bright_setup(key)
    inner = jax.random.fold_in(key, 23)
    base = jax.random.truncated_normal(inner, -3.0, 3.0, (K, S * 2 * NA), jnp.float32)
    return (base * amplitude[:, None]).astype(jnp.bfloat16)


def draw_ctf(key, part):
    return jax.random.uniform(jax.random.fold_in(key, 24), (NP, S * NA), jnp.float32, -1.0, 1.0).astype(jnp.bfloat16)


def draw_images(key, part):
    placement, class_lists = routing_tables(key)
    is_bright, amplitude = bright_setup(key)
    inner = jax.random.fold_in(key, 25)
    noise = jax.random.truncated_normal(inner, -6.0, 6.0, (NP, S, 2, NA), jnp.float32)
    rows = placement[class_lists]
    hit = is_bright[rows]
    has_bright = jnp.any(hit, axis=1)
    first = jnp.argmax(hit.astype(jnp.int32), axis=1)
    row_pick = jnp.take_along_axis(rows, first[:, None], axis=1)[:, 0]
    table = draw_references(key, part).reshape(K, S, 2, NA)
    picked = table[row_pick]
    turn_by = jax.random.randint(jax.random.fold_in(key, 26), (NP,), 0, NA)
    index = (jnp.arange(NA, dtype=jnp.int32)[None, :] - turn_by[:, None]) % NA
    turned = jnp.take_along_axis(picked, index[:, None, None, :], axis=3)
    ctf_values = draw_ctf(key, part).reshape(NP, S, NA)
    aligned = ctf_values[:, :, None, :] * turned
    images = noise + jnp.where(has_bright[:, None, None, None], aligned, 0.0)
    return images.reshape(NP, S * 2 * NA).astype(jnp.bfloat16)


def setup_inputs(seed: int = 0) -> dict:
    streams_of = jax.random.split(jax.random.key(seed), 7)
    return {
        "images": draw_images(jax.random.fold_in(streams_of[6], 71), 0),
        "ctf": draw_ctf(jax.random.fold_in(streams_of[6], 71), 0),
        "classes": draw_classes(jax.random.fold_in(streams_of[6], 71), 0),
        "class_place": draw_class_place(jax.random.fold_in(streams_of[6], 71), 0),
        "references": draw_references(jax.random.fold_in(streams_of[6], 71), 0),
        "sigma2": draw_sigma2(jax.random.fold_in(streams_of[6], 71), 0),
    }


def reference(images, ctf, classes, class_place, references, sigma2):
    shells = sigma2.shape[0]
    angles = ctf.shape[1] // shells
    class_total = class_place.shape[0]
    ref_table = references.astype(jnp.float32).reshape(class_total, shells, 2, angles)
    ref_power = jnp.sum(ref_table * ref_table, axis=2).astype(jnp.bfloat16)
    ref_power = lax.optimization_barrier(ref_power).astype(jnp.float32)
    table_hat = jnp.fft.rfft(ref_table, axis=-1)
    power_hat = jnp.fft.rfft(ref_power, axis=-1)
    table_rows = class_place[classes].astype(jnp.int32)
    inverse_sigma = 1.0 / sigma2
    block_count = 32
    block_rows = images.shape[0] // block_count
    num_zero = jnp.zeros(table_hat.shape, table_hat.dtype)
    den_zero = jnp.zeros(power_hat.shape, power_hat.dtype)

    def advance(carry, block_data):
        num_hat, den_hat = carry
        image_block, ctf_block, rows_block = block_data
        scaling = ctf_block.astype(jnp.float32).reshape(block_rows, shells, angles) * inverse_sigma[None, :, None]
        weighted = (image_block.astype(jnp.float32).reshape(block_rows, shells, 2, angles) * scaling[:, :, None, :]).astype(jnp.bfloat16)
        ctf_power = (ctf_block.astype(jnp.float32).reshape(block_rows, shells, angles) * scaling).astype(jnp.bfloat16)
        weighted, ctf_power = lax.optimization_barrier((weighted, ctf_power))
        weighted_hat = jnp.fft.rfft(weighted.astype(jnp.float32), axis=-1)
        ctf_hat = jnp.fft.rfft(ctf_power.astype(jnp.float32), axis=-1)
        ref_rows = table_hat[rows_block]
        pow_rows = power_hat[rows_block]
        cross_term = jnp.fft.irfft(jnp.sum(weighted_hat[:, None] * jnp.conj(ref_rows), axis=(2, 3)), n=angles, axis=-1)
        quad_term = jnp.fft.irfft(jnp.sum(ctf_hat[:, None] * jnp.conj(pow_rows), axis=2), n=angles, axis=-1)
        logits = cross_term - 0.5 * quad_term
        highest = jnp.max(logits, axis=(1, 2), keepdims=True)
        exponent = jnp.exp(logits - highest)
        posterior = (exponent / jnp.sum(exponent, axis=(1, 2), keepdims=True)).astype(jnp.bfloat16)
        posterior = lax.optimization_barrier(posterior).astype(jnp.float32)
        post_hat = jnp.conj(jnp.fft.rfft(posterior, axis=-1))
        num_hat = num_hat.at[rows_block].add(weighted_hat[:, None] * post_hat[:, :, None, None, :])
        den_hat = den_hat.at[rows_block].add(ctf_hat[:, None] * post_hat[:, :, None, :])
        return (num_hat, den_hat), None

    block_data = (images.reshape(block_count, block_rows, -1), ctf.reshape(block_count, block_rows, -1), table_rows.reshape(block_count, block_rows, -1))
    (num_hat, den_hat), unused = lax.scan(advance, (num_zero, den_zero), block_data)
    numerator = jnp.fft.irfft(num_hat, n=angles, axis=-1)
    denominator = jnp.fft.irfft(den_hat, n=angles, axis=-1)
    updated = numerator / (denominator[:, :, None, :] + 1.0)
    return updated.reshape(class_total, -1)
```

```python
import jax
import jax.numpy as jnp
import numpy as np
from jax import lax
from jax.experimental import pallas as pl
from jax.experimental.pallas import tpu as pltpu
from jax.sharding import PartitionSpec as P

TOP = 4
NA = 72
HALF = 64
LANES = 128
PITCH = 16
SHELLS = 8
PAIR = 2 * NA
IMG_W = SHELLS * PAIR
CTF_W = SHELLS * NA
ROW_W = IMG_W + CTF_W
SEND_W = 1792
FREQS = NA // 2 + 1
TOPPAD = 112
TABLE = 384

bf16 = jnp.bfloat16
f32 = jnp.float32


def split3(x):
    x = np.asarray(x, np.float32)
    hi = x.astype(bf16)
    rest = x - hi.astype(np.float32)
    mid = rest.astype(bf16)
    low = (rest - mid.astype(np.float32)).astype(bf16)
    return np.stack([hi, mid, low])


def make_tables():
    freq = np.arange(FREQS)
    angle = np.arange(NA)
    phase = (freq[None, :] * angle[:, None]) % NA * (2.0 * np.pi / NA)
    cos, sin = np.cos(phase), np.sin(phase)
    weight = np.where((freq == 0) | (freq == NA // 2), 1.0, 2.0) / NA
    forward = np.zeros((TABLE, 2 * LANES))
    inverse = np.zeros((TABLE, 2 * LANES))
    even = np.zeros((TABLE, 2 * LANES))
    odd = np.zeros((TABLE, 2 * LANES))
    both = np.zeros((LANES, 2 * LANES))
    logit = np.zeros((2 * LANES, LANES))
    for part in range(2):
        rows = slice(TOPPAD + part * NA, TOPPAD + part * NA + NA)
        first = slice(TOPPAD, TOPPAD + NA)
        re = slice(part * HALF, part * HALF + FREQS)
        im = slice(LANES + part * HALF, LANES + part * HALF + FREQS)
        forward[rows, re], forward[rows, im] = cos, -sin
        inverse[rows, re], inverse[rows, im] = cos * weight, -sin * weight
        side = odd if part else even
        side[first, re], side[first, im] = -0.5 * cos, 0.5 * sin
        both[:NA, re], both[:NA, im] = cos, -sin
        logit[re, :NA], logit[im, :NA] = (cos * weight).T, (-sin * weight).T
    lane = np.arange(IMG_W)
    source = NA * (lane // PAIR) + lane % NA
    spread = (np.arange(CTF_W)[:, None] == source[None, :]).astype(bf16)
    return (
        split3(forward),
        np.stack([split3(even), split3(odd)]),
        split3(inverse)[:2],
        split3(both),
        logit.astype(np.float32),
        spread,
    )


def dot(a, b):
    return lax.dot_general(a, b, (((1,), (0,)), ((), ())), preferred_element_type=f32)


def dot_t(a, b):
    return lax.dot_general(a, b, (((1,), (1,)), ((), ())), preferred_element_type=f32)


def window(table_ref, lead, index):
    start = TOPPAD - 16 * index
    return table_ref[(*lead, slice(start, start + 2 * LANES), slice(None))]


def pack_kernel(img_ref, images, ctf, classes, place, refs, wsend, rsend):
    rows = []
    lane = lax.broadcasted_iota(jnp.int32, (16, 64), 1)
    for j in range(TOP):
        hit = classes[:, j : j + 1] == lax.broadcasted_iota(jnp.int32, (16, 224), 1)
        rows.append(jnp.sum(jnp.where(hit, place[...], 0), axis=1, keepdims=True))
    listed = jnp.zeros((16, 64), f32)
    for j in range(TOP):
        listed = jnp.where(lane == j, rows[j].astype(f32), listed)
    tail = listed.astype(bf16)
    for d in range(8):
        wsend[d, :, :IMG_W] = images[:, d * IMG_W : (d + 1) * IMG_W]
        wsend[d, :, IMG_W:] = jnp.concatenate(
            [ctf[:, d * CTF_W : (d + 1) * CTF_W], tail], axis=1
        )
    start = pl.multiple_of(img_ref[0] * IMG_W, LANES)
    mine = refs[:, pl.ds(start, IMG_W)].astype(f32)
    mine = jnp.concatenate([mine, jnp.zeros((1, IMG_W), f32)], axis=0).astype(bf16)
    for o in range(32):
        rsend[o] = mine


def weigh_kernel(recv, inv, spread, fwd, wre, wim):
    ctf = recv[:, IMG_W:ROW_W]
    ctf32 = ctf.astype(f32)
    power = (ctf32 * (ctf32 * inv[:, IMG_W:ROW_W])).astype(bf16)
    power = jnp.concatenate([power, jnp.zeros((LANES, 64), bf16)], axis=1)
    scale = dot(ctf, spread[...]) * inv[:, :IMG_W]
    weighted = (recv[:, :IMG_W].astype(f32) * scale).astype(bf16)
    count = recv.shape[0]
    for s in range(SHELLS + 4):
        if s < SHELLS:
            x = weighted[:, LANES * s : LANES * s + 2 * LANES]
            index = s
        else:
            index = s - SHELLS
            x = power[:, LANES * index : LANES * index + 2 * LANES]
        y = dot(x, window(fwd, (0,), index))
        y += dot(x, window(fwd, (1,), index))
        y += dot(x, window(fwd, (2,), index))
        wre[pl.ds(s, count, stride=PITCH), :] = y[:, :LANES]
        wim[pl.ds(s, count, stride=PITCH), :] = y[:, LANES:]
    zero = jnp.zeros((count, LANES), f32)
    for s in range(SHELLS + 4, PITCH):
        wre[pl.ds(s, count, stride=PITCH), :] = zero
        wim[pl.ds(s, count, stride=PITCH), :] = zero


def score_kernel(idx, recv, fwd, side, logit, wre, wim, out, rre, rim, pq):
    count = 256
    raw32 = recv[...].astype(f32).reshape(count, IMG_W)
    raw = raw32.astype(bf16)
    square = raw32 * raw32
    shifted = jnp.concatenate([square[:, NA:], square[:, :NA]], axis=1)
    power = (square + shifted).astype(bf16)
    for s in range(SHELLS):
        x = raw[:, LANES * s : LANES * s + 2 * LANES]
        y = dot(x, window(fwd, (0,), s))
        y += dot(x, window(fwd, (1,), s))
        y += dot(x, window(fwd, (2,), s))
        rre[pl.ds(s, count, stride=PITCH), :] = y[:, :LANES]
        rim[pl.ds(s, count, stride=PITCH), :] = y[:, LANES:]
    for j in range(SHELLS // 2):
        y = jnp.zeros((count, 2 * LANES), f32)
        for parity in range(2):
            s = 2 * j + parity
            x = power[:, LANES * s : LANES * s + 2 * LANES]
            for k in range(3):
                y += dot(x, window(side, (parity, k), s))
        rre[pl.ds(SHELLS + j, count, stride=PITCH), :] = y[:, :LANES]
        rim[pl.ds(SHELLS + j, count, stride=PITCH), :] = y[:, LANES:]
    zero = jnp.zeros((count, LANES), f32)
    for s in range(SHELLS + 4, PITCH):
        rre[pl.ds(s, count, stride=PITCH), :] = zero
        rim[pl.ds(s, count, stride=PITCH), :] = zero

    def block(b, carry):
        rows = [[[], []] for _ in range(TOP)]
        for u in range(8):
            i = b * 8 + u
            at = pl.multiple_of(i * PITCH, PITCH)
            a_re = wre[pl.ds(at, PITCH), :]
            a_im = wim[pl.ds(at, PITCH), :]
            for j in range(TOP):
                t = pl.multiple_of(idx[i * TOP + j] * PITCH, PITCH)
                b_re = rre[pl.ds(t, PITCH), :]
                b_im = rim[pl.ds(t, PITCH), :]
                p = a_re * b_re + a_im * b_im
                q = a_im * b_re - a_re * b_im
                rows[j][0].append(jnp.sum(p, axis=0, keepdims=True))
                rows[j][1].append(jnp.sum(q, axis=0, keepdims=True))
        at = pl.multiple_of(b * 8, 8)
        for j in range(TOP):
            pq[j, pl.ds(at, 8), :LANES] = jnp.concatenate(rows[j][0], axis=0)
            pq[j, pl.ds(at, 8), LANES:] = jnp.concatenate(rows[j][1], axis=0)
        return carry

    lax.fori_loop(0, 16, block, 0)
    for j in range(TOP):
        out[:, LANES * j : LANES * j + LANES] = lax.dot_general(
            pq[j],
            logit[...],
            (((1,), (0,)), ((), ())),
            precision=lax.Precision.HIGHEST,
            preferred_element_type=f32,
        )


def softmax_kernel(parts, out):
    logits = parts[0]
    for k in range(1, 8):
        logits += parts[k]
    lane = lax.broadcasted_iota(jnp.int32, logits.shape, 1)
    valid = lane % LANES < NA
    logits = jnp.where(valid, logits, -jnp.inf)
    highest = jnp.max(logits, axis=1, keepdims=True)
    e = jnp.exp(logits - highest)
    posterior = (e / jnp.sum(e, axis=1, keepdims=True)).astype(bf16)
    for k in range(8):
        out[k] = posterior


def gather_kernel(idx, post, both, inverse, wre, wim, out, gre, gim, are, aim, total):
    for j in range(TOP):
        x = post[:, LANES * j : LANES * j + LANES]
        y = dot(x, both[0]) + dot(x, both[1]) + dot(x, both[2])
        gre[j] = y[:, :LANES]
        gim[j] = y[:, LANES:]
    are[...] = jnp.zeros_like(are)
    aim[...] = jnp.zeros_like(aim)

    def block(b, carry):
        for u in range(4):
            i = b * 4 + u
            at = pl.multiple_of(i * PITCH, PITCH)
            a_re = wre[pl.ds(at, PITCH), :]
            a_im = wim[pl.ds(at, PITCH), :]
            places, sums = [], []
            for j in range(TOP):
                t = pl.multiple_of(idx[i * TOP + j] * PITCH, PITCH)
                g_re = gre[j, pl.ds(i, 1), :]
                g_im = gim[j, pl.ds(i, 1), :]
                places.append(t)
                sums.append(
                    (
                        are[pl.ds(t, PITCH), :] + (a_re * g_re + a_im * g_im),
                        aim[pl.ds(t, PITCH), :] + (a_im * g_re - a_re * g_im),
                    )
                )
            for j in range(TOP):
                are[pl.ds(places[j], PITCH), :] = sums[j][0]
                aim[pl.ds(places[j], PITCH), :] = sums[j][1]
        return carry

    lax.fori_loop(0, 32, block, 0)
    count = 256
    total[...] = jnp.zeros_like(total)
    for s in range(SHELLS + 4):
        index = s if s < SHELLS else s - SHELLS
        base = LANES * s if s < SHELLS else IMG_W + LANES * index
        x = jnp.concatenate(
            [are[pl.ds(s, count, stride=PITCH), :], aim[pl.ds(s, count, stride=PITCH), :]], axis=1
        )
        hi = x.astype(bf16)
        low = (x - hi.astype(f32)).astype(bf16)
        t_hi, t_low = window(inverse, (0,), index), window(inverse, (1,), index)
        y = dot_t(hi, t_hi) + dot_t(low, t_hi) + dot_t(hi, t_low)
        total[:, base : base + 2 * LANES] += y
    out[...] = total[...].reshape(32, 8, SEND_W).astype(bf16)


def final_kernel(parts, spread, out):
    total = parts[0].astype(f32)
    for k in range(1, 32):
        total += parts[k].astype(f32)
    below = lax.dot_general(
        total[:, IMG_W:ROW_W] + 1.0,
        spread[...].astype(f32),
        (((1,), (0,)), ((), ())),
        precision=lax.Precision.HIGHEST,
        preferred_element_type=f32,
    )
    out[...] = (total[:, :IMG_W] / below)[:7]


VM = pl.BlockSpec(memory_space=pltpu.VMEM)
SM = pl.BlockSpec(memory_space=pltpu.SMEM)
PARAMS = pltpu.CompilerParams(vmem_limit_bytes=56 * 1024 * 1024)


def on_device(images, ctf, classes, class_place, references, sigma2):
    fwd, side, inverse, both, logit, spread = make_tables()
    img = lax.axis_index("img")
    wsend, rsend = pl.pallas_call(
        pack_kernel,
        out_shape=(
            jax.ShapeDtypeStruct((8, 16, SEND_W), bf16),
            jax.ShapeDtypeStruct((32, 8, IMG_W), bf16),
        ),
        in_specs=[SM, VM, VM, VM, VM, VM],
        out_specs=(VM, VM),
        compiler_params=PARAMS,
        name="pack",
    )(img.reshape(1), images, ctf, classes, class_place.reshape(1, -1), references)
    wrecv = lax.all_to_all(wsend, "img", 0, 0, tiled=True).reshape(128, SEND_W)
    rrecv = lax.all_to_all(rsend, "cls", 0, 0, tiled=True)
    table_rows = wrecv[:, ROW_W : ROW_W + TOP].astype(jnp.int32)
    idx = (table_rows // 7 * 8 + table_rows % 7).reshape(-1)
    inv = 1.0 / lax.dynamic_slice(sigma2, (img * SHELLS,), (SHELLS,))
    inv = jnp.concatenate([jnp.repeat(inv, PAIR), jnp.repeat(inv, NA)]).reshape(1, ROW_W)
    hat = jax.ShapeDtypeStruct((128 * PITCH, LANES), f32)
    wre, wim = pl.pallas_call(
        weigh_kernel,
        out_shape=(hat, hat),
        in_specs=[VM] * 4,
        out_specs=(VM, VM),
        compiler_params=PARAMS,
        name="weigh",
    )(wrecv, inv, spread, fwd)
    partial = pl.pallas_call(
        score_kernel,
        out_shape=jax.ShapeDtypeStruct((128, TOP * LANES), f32),
        in_specs=[SM] + [VM] * 6,
        out_specs=VM,
        scratch_shapes=[
            pltpu.VMEM((256 * PITCH, LANES), f32),
            pltpu.VMEM((256 * PITCH, LANES), f32),
            pltpu.VMEM((TOP, 128, 2 * LANES), f32),
        ],
        compiler_params=PARAMS,
        name="score",
    )(idx, rrecv, fwd, side, logit, wre, wim)
    parts = lax.all_to_all(partial.reshape(8, 16, TOP * LANES), "img", 0, 0, tiled=True)
    post = pl.pallas_call(
        softmax_kernel,
        out_shape=jax.ShapeDtypeStruct((8, 16, TOP * LANES), bf16),
        in_specs=[VM],
        out_specs=VM,
        compiler_params=PARAMS,
        name="softmax",
    )(parts)
    post = lax.all_to_all(post, "img", 0, 0, tiled=True).reshape(128, TOP * LANES)
    sums = pl.pallas_call(
        gather_kernel,
        out_shape=jax.ShapeDtypeStruct((32, 8, SEND_W), bf16),
        in_specs=[SM] + [VM] * 5,
        out_specs=VM,
        scratch_shapes=[
            pltpu.VMEM((TOP, 128, LANES), f32),
            pltpu.VMEM((TOP, 128, LANES), f32),
            pltpu.VMEM((256 * PITCH, LANES), f32),
            pltpu.VMEM((256 * PITCH, LANES), f32),
            pltpu.VMEM((256, SEND_W), f32),
        ],
        compiler_params=PARAMS,
        name="gather",
    )(idx, post, both, inverse, wre, wim)
    arrived = lax.all_to_all(sums, "cls", 0, 0, tiled=True)
    return pl.pallas_call(
        final_kernel,
        out_shape=jax.ShapeDtypeStruct((7, IMG_W), f32),
        in_specs=[VM, VM],
        out_specs=VM,
        compiler_params=PARAMS,
        name="final",
    )(arrived, spread)


def solution(mesh):
    in_specs = (
        P(("cls", "img"), None),
        P(("cls", "img"), None),
        P(("cls", "img"), None),
        P(),
        P("cls", None),
        P(),
    )
    return jax.shard_map(
        on_device, mesh=mesh, in_specs=in_specs, out_specs=P("cls", "img"), check_vma=False
    )
```

```python
import jax
import jax.numpy as jnp
import numpy as np
from jax import lax
from jax.experimental import pallas as pl
from jax.experimental.pallas import tpu as pltpu
from jax.sharding import Mesh
from jax.sharding import PartitionSpec as P

TOP = 4
NA = 72
HALF = 64
LANES = 128
PITCH = 8
SHELLS = 4
WINDOWS = 6
MEMBERS = 16
PARTICLES = 16 * MEMBERS
OWNERS = 32
TABLE_ROWS = 8 * OWNERS
PAIR = 2 * NA
IMG_W = SHELLS * PAIR
CTF_W = SHELLS * NA
REF_W = 640
ROW_W = IMG_W + CTF_W
SEND_W = 896
LOGIT_W = 384
FREQS = NA // 2 + 1
TOPPAD = 112
TABLE = 384
CLS = ("xh", "xl", "z")
GROUP = ("xl", "img")
DEVICES = ("xh", "xl", "z", "img")

bf16 = jnp.bfloat16
f32 = jnp.float32


def split3(x):
    x = np.asarray(x, np.float32)
    hi = x.astype(bf16)
    rest = x - hi.astype(np.float32)
    mid = rest.astype(bf16)
    low = (rest - mid.astype(np.float32)).astype(bf16)
    return np.stack([hi, mid, low])


def make_tables():
    freq = np.arange(FREQS)
    angle = np.arange(NA)
    phase = (freq[None, :] * angle[:, None]) % NA * (2.0 * np.pi / NA)
    cos, sin = np.cos(phase), np.sin(phase)
    weight = np.where((freq == 0) | (freq == NA // 2), 1.0, 2.0) / NA
    forward = np.zeros((TABLE, 2 * LANES))
    inverse = np.zeros((TABLE, 2 * LANES))
    side = np.zeros((2, TABLE, 2 * LANES))
    both = np.zeros((2, TABLE, 2 * LANES))
    logit = np.zeros((2 * LANES, LANES))
    first = slice(TOPPAD, TOPPAD + NA)
    for part in range(2):
        rows = slice(TOPPAD + part * NA, TOPPAD + part * NA + NA)
        re = slice(part * HALF, part * HALF + FREQS)
        im = slice(LANES + part * HALF, LANES + part * HALF + FREQS)
        forward[rows, re], forward[rows, im] = cos, -sin
        inverse[rows, re], inverse[rows, im] = cos * weight, -sin * weight
        side[part, first, re], side[part, first, im] = -0.5 * cos, 0.5 * sin
        for second in range(2):
            at = slice(TOPPAD + second * NA, TOPPAD + second * NA + NA)
            both[second, at, re], both[second, at, im] = cos, -sin
        logit[re, :NA], logit[im, :NA] = (cos * weight).T, (-sin * weight).T
    lane = np.arange(SEND_W)
    source = np.where(lane < IMG_W, IMG_W + NA * (lane // PAIR) + lane % NA, lane) - 512
    spread = (np.arange(384)[:, None] == source[None, :]) & (lane < ROW_W)[None, :]
    below = (np.arange(384)[:, None] == source[None, :]) & (lane < IMG_W)[None, :]
    return (
        split3(forward),
        np.stack([split3(side[0]), split3(side[1])]),
        split3(inverse)[:2],
        np.stack([split3(both[0])[:2], split3(both[1])[:2]]),
        logit.astype(np.float32),
        spread.astype(bf16),
        below[:, :REF_W].astype(bf16),
    )


def dot(a, b):
    return lax.dot_general(a, b, (((1,), (0,)), ((), ())), preferred_element_type=f32)


def dot_t(a, b):
    return lax.dot_general(a, b, (((1,), (1,)), ((), ())), preferred_element_type=f32)


def dot_exact(a, b):
    return lax.dot_general(
        a,
        b,
        (((1,), (0,)), ((), ())),
        precision=lax.Precision.HIGHEST,
        preferred_element_type=f32,
    )


def window(table_ref, lead, index):
    start = TOPPAD - 16 * index
    return table_ref[(*lead, slice(start, start + 2 * LANES), slice(None))]


def lanes_of(x, index):
    return x[:, LANES * index : LANES * index + 2 * LANES]


def pack_kernel(at_ref, images, ctf, classes, place, refs, wsend, rsend):
    lane = lax.broadcasted_iota(jnp.int32, (16, SEND_W - ROW_W), 1)
    listed = jnp.zeros((16, SEND_W - ROW_W), f32)
    for j in range(TOP):
        hit = classes[:, j : j + 1] == lax.broadcasted_iota(jnp.int32, (16, 224), 1)
        row = jnp.sum(jnp.where(hit, place[...], 0), axis=1, keepdims=True)
        listed = jnp.where(lane == j, row.astype(f32), listed)
    tail = listed.astype(bf16)
    for h in range(2):
        for i in range(8):
            shell = i * 8 + h * SHELLS
            wsend[h * 8 + i] = jnp.concatenate(
                [
                    images[:, shell * PAIR : shell * PAIR + IMG_W],
                    ctf[:, shell * NA : shell * NA + CTF_W],
                    tail,
                ],
                axis=1,
            )
    start = pl.multiple_of(at_ref[0] * 2 * IMG_W, LANES)
    mine = refs[:, pl.ds(start, 2 * IMG_W)].astype(f32)
    for h in range(2):
        half = mine[:, h * IMG_W : (h + 1) * IMG_W]
        half = jnp.concatenate([half, jnp.zeros((7, REF_W - IMG_W), f32)], axis=1)
        half = jnp.concatenate([half, jnp.zeros((1, REF_W), f32)], axis=0).astype(bf16)
        for o in range(OWNERS):
            if (o // 8) % 2 == h:
                rsend[o] = half


def weigh_kernel(recv, inv, spread, fwd, wre, wim):
    scale = dot(recv[:, 512:], spread[...]) * inv[...]
    weighted = (recv[...].astype(f32) * scale).astype(bf16)
    for s in range(WINDOWS):
        x = lanes_of(weighted, s)
        y = sum(dot(x, window(fwd, (k,), s)) for k in range(3))
        wre[pl.ds(s, PARTICLES, stride=PITCH), :] = y[:, :LANES]
        wim[pl.ds(s, PARTICLES, stride=PITCH), :] = y[:, LANES:]
    zero = jnp.zeros((PARTICLES, LANES), f32)
    for s in range(WINDOWS, PITCH):
        wre[pl.ds(s, PARTICLES, stride=PITCH), :] = zero
        wim[pl.ds(s, PARTICLES, stride=PITCH), :] = zero


def score_kernel(idx, recv, fwd, side, logit, wre, wim, out, rre, rim, pq):
    raw32 = recv[...].astype(f32).reshape(TABLE_ROWS, REF_W)
    raw = raw32.astype(bf16)
    square = raw32 * raw32
    shifted = jnp.concatenate([square[:, NA:], square[:, :NA]], axis=1)
    power = (square + shifted).astype(bf16)
    for s in range(SHELLS):
        y = sum(dot(lanes_of(raw, s), window(fwd, (k,), s)) for k in range(3))
        rre[pl.ds(s, TABLE_ROWS, stride=PITCH), :] = y[:, :LANES]
        rim[pl.ds(s, TABLE_ROWS, stride=PITCH), :] = y[:, LANES:]
    for j in range(SHELLS // 2):
        y = sum(
            dot(lanes_of(power, 2 * j + parity), window(side, (parity, k), 2 * j + parity))
            for parity in range(2)
            for k in range(3)
        )
        rre[pl.ds(SHELLS + j, TABLE_ROWS, stride=PITCH), :] = y[:, :LANES]
        rim[pl.ds(SHELLS + j, TABLE_ROWS, stride=PITCH), :] = y[:, LANES:]
    zero = jnp.zeros((TABLE_ROWS, LANES), f32)
    for s in range(WINDOWS, PITCH):
        rre[pl.ds(s, TABLE_ROWS, stride=PITCH), :] = zero
        rim[pl.ds(s, TABLE_ROWS, stride=PITCH), :] = zero

    def block(b, carry):
        rows = [[[], []] for _ in range(TOP)]
        for u in range(8):
            i = b * 8 + u
            at = pl.multiple_of(i * PITCH, PITCH)
            a_re = wre[pl.ds(at, PITCH), :]
            a_im = wim[pl.ds(at, PITCH), :]
            for j in range(TOP):
                t = pl.multiple_of(idx[i * TOP + j] * PITCH, PITCH)
                b_re = rre[pl.ds(t, PITCH), :]
                b_im = rim[pl.ds(t, PITCH), :]
                p = a_re * b_re + a_im * b_im
                q = a_im * b_re - a_re * b_im
                rows[j][0].append(jnp.sum(p, axis=0, keepdims=True))
                rows[j][1].append(jnp.sum(q, axis=0, keepdims=True))
        at = pl.multiple_of(b * 8, 8)
        for j in range(TOP):
            pq[j, pl.ds(at, 8), :LANES] = jnp.concatenate(rows[j][0], axis=0)
            pq[j, pl.ds(at, 8), LANES:] = jnp.concatenate(rows[j][1], axis=0)
        return carry

    lax.fori_loop(0, PARTICLES // 8, block, 0)
    logits = [dot_exact(pq[j], logit[...])[:, :NA] for j in range(TOP)]
    logits.append(jnp.zeros((PARTICLES, LOGIT_W - TOP * NA), f32))
    out[...] = jnp.concatenate(logits, axis=1)


def softmax_kernel(parts, out):
    logits = parts[0]
    for k in range(1, MEMBERS):
        logits += parts[k]
    lane = lax.broadcasted_iota(jnp.int32, logits.shape, 1)
    logits = jnp.where(lane < TOP * NA, logits, -jnp.inf)
    highest = jnp.max(logits, axis=1, keepdims=True)
    e = jnp.exp(logits - highest)
    posterior = (e / jnp.sum(e, axis=1, keepdims=True)).astype(bf16)
    for k in range(MEMBERS):
        out[k] = posterior


def gather_kernel(idx, post, both, inverse, wre, wim, out, gre, gim, are, aim, total):
    for j in range(TOP):
        x = lanes_of(post, j // 2)
        y = sum(dot(x, window(both, (j % 2, k), j // 2)) for k in range(2))
        gre[j] = y[:, :LANES]
        gim[j] = y[:, LANES:]
    are[...] = jnp.zeros_like(are)
    aim[...] = jnp.zeros_like(aim)

    def block(b, carry):
        for u in range(4):
            i = b * 4 + u
            at = pl.multiple_of(i * PITCH, PITCH)
            a_re = wre[pl.ds(at, PITCH), :]
            a_im = wim[pl.ds(at, PITCH), :]
            places, sums = [], []
            for j in range(TOP):
                t = pl.multiple_of(idx[i * TOP + j] * PITCH, PITCH)
                g_re = gre[j, pl.ds(i, 1), :]
                g_im = gim[j, pl.ds(i, 1), :]
                places.append(t)
                sums.append(
                    (
                        are[pl.ds(t, PITCH), :] + (a_re * g_re + a_im * g_im),
                        aim[pl.ds(t, PITCH), :] + (a_im * g_re - a_re * g_im),
                    )
                )
            for j in range(TOP):
                are[pl.ds(places[j], PITCH), :] = sums[j][0]
                aim[pl.ds(places[j], PITCH), :] = sums[j][1]
        return carry

    lax.fori_loop(0, PARTICLES // 4, block, 0)
    total[...] = jnp.zeros_like(total)
    for s in range(WINDOWS):
        x = jnp.concatenate(
            [
                are[pl.ds(s, TABLE_ROWS, stride=PITCH), :],
                aim[pl.ds(s, TABLE_ROWS, stride=PITCH), :],
            ],
            axis=1,
        )
        hi = x.astype(bf16)
        low = (x - hi.astype(f32)).astype(bf16)
        t_hi, t_low = window(inverse, (0,), s), window(inverse, (1,), s)
        total[:, LANES * s : LANES * s + 2 * LANES] += (
            dot_t(hi, t_hi) + dot_t(low, t_hi) + dot_t(hi, t_low)
        )
    out[...] = total[...].reshape(OWNERS, 8, SEND_W).astype(bf16)


def final_kernel(parts, below, out):
    sums = []
    for h in range(2):
        members = [s for s in range(OWNERS) if (s // 8) % 2 == h]
        total = parts[members[0]].astype(f32)
        for s in members[1:]:
            total += parts[s].astype(f32)
        sums.append(total)
    total = jnp.concatenate(sums, axis=0)
    under = dot_exact(total[:, 512:] + 1.0, below[...].astype(f32))[:, :IMG_W]
    new = total[:, :IMG_W] / under
    out[:, :IMG_W] = new[:7]
    out[:, IMG_W:] = new[8:15]


VM = pl.BlockSpec(memory_space=pltpu.VMEM)
SM = pl.BlockSpec(memory_space=pltpu.SMEM)
PARAMS = pltpu.CompilerParams(vmem_limit_bytes=24 * 1024 * 1024)


def call(kernel, name, out_shape, in_specs, args, scratch=()):
    out_specs = tuple(VM for _ in out_shape) if isinstance(out_shape, tuple) else VM
    return pl.pallas_call(
        kernel,
        out_shape=out_shape,
        in_specs=in_specs,
        out_specs=out_specs,
        scratch_shapes=scratch,
        compiler_params=PARAMS,
        name=name,
    )(*args)


def on_device(images, ctf, classes, class_place, references, sigma2):
    fwd, side, inverse, both, logit, spread, below = make_tables()
    img, h = lax.axis_index("img"), lax.axis_index("xl")
    shape = jax.ShapeDtypeStruct
    wsend, rsend = call(
        pack_kernel,
        "pack",
        (shape((MEMBERS, 16, SEND_W), bf16), shape((OWNERS, 8, REF_W), bf16)),
        [SM] + [VM] * 5,
        (img.reshape(1), images, ctf, classes, class_place.reshape(1, -1), references),
    )
    wrecv = lax.all_to_all(wsend, GROUP, 0, 0, tiled=True).reshape(PARTICLES, SEND_W)
    rrecv = lax.all_to_all(rsend, CLS, 0, 0, tiled=True)
    table_rows = wrecv[:, ROW_W : ROW_W + TOP].astype(jnp.int32)
    idx = (table_rows // 7 * 8 + table_rows % 7).reshape(-1)
    inv = 1.0 / lax.dynamic_slice(sigma2, (img * 8 + h * SHELLS,), (SHELLS,))
    inv = jnp.concatenate(
        [jnp.repeat(inv, PAIR), jnp.repeat(inv, NA), jnp.zeros((SEND_W - ROW_W,), f32)]
    ).reshape(1, SEND_W)
    hat = shape((PARTICLES * PITCH, LANES), f32)
    wre, wim = call(weigh_kernel, "weigh", (hat, hat), [VM] * 4, (wrecv, inv, spread, fwd))
    table = pltpu.VMEM((TABLE_ROWS * PITCH, LANES), f32)
    partial = call(
        score_kernel,
        "score",
        shape((PARTICLES, LOGIT_W), f32),
        [SM] + [VM] * 6,
        (idx, rrecv, fwd, side, logit, wre, wim),
        [table, table, pltpu.VMEM((TOP, PARTICLES, 2 * LANES), f32)],
    )
    parts = lax.all_to_all(partial.reshape(MEMBERS, 16, LOGIT_W), GROUP, 0, 0, tiled=True)
    post = call(
        softmax_kernel, "softmax", shape((MEMBERS, 16, LOGIT_W), bf16), [VM], (parts,)
    )
    post = lax.all_to_all(post, GROUP, 0, 0, tiled=True).reshape(PARTICLES, LOGIT_W)
    each = pltpu.VMEM((TOP, PARTICLES, LANES), f32)
    sums = call(
        gather_kernel,
        "gather",
        shape((OWNERS, 8, SEND_W), bf16),
        [SM] + [VM] * 5,
        (idx, post, both, inverse, wre, wim),
        [each, each, table, table, pltpu.VMEM((TABLE_ROWS, SEND_W), f32)],
    )
    arrived = lax.all_to_all(sums, CLS, 0, 0, tiled=True)
    return call(
        final_kernel, "final", shape((7, 2 * IMG_W), f32), [VM, VM], (arrived, below)
    )


def solution(mesh):
    finer = Mesh(mesh.devices.reshape(2, 2, 8, 8), DEVICES)
    in_specs = (
        P(DEVICES, None),
        P(DEVICES, None),
        P(DEVICES, None),
        P(),
        P(CLS, None),
        P(),
    )
    return jax.shard_map(
        on_device, mesh=finer, in_specs=in_specs, out_specs=P(CLS, "img"), check_vma=False
    )
```

```python
import jax
import jax.numpy as jnp
import numpy as np
from jax import lax
from jax.experimental import pallas as pl
from jax.experimental.pallas import tpu as pltpu
from jax.sharding import Mesh
from jax.sharding import PartitionSpec as P

TOP = 4
NA = 72
HALF = 64
LANES = 128
PITCH = 8
SHELLS = 4
WINDOWS = 6
MEMBERS = 16
PARTICLES = 16 * MEMBERS
OWNERS = 32
TABLE_ROWS = 8 * OWNERS
PAIR = 2 * NA
IMG_W = SHELLS * PAIR
CTF_W = SHELLS * NA
REF_W = 640
ROW_W = IMG_W + CTF_W
SEND_W = 896
LOGIT_W = 384
FREQS = NA // 2 + 1
TOPPAD = 112
TABLE = 384
CLS = ("xh", "xl", "z")
GROUP = ("xl", "img")
DEVICES = ("xh", "xl", "z", "img")

bf16 = jnp.bfloat16
f32 = jnp.float32


def split3(x):
    x = np.asarray(x, np.float32)
    hi = x.astype(bf16)
    rest = x - hi.astype(np.float32)
    mid = rest.astype(bf16)
    low = (rest - mid.astype(np.float32)).astype(bf16)
    return np.stack([hi, mid, low])


def make_tables():
    freq = np.arange(FREQS)
    angle = np.arange(NA)
    phase = (freq[None, :] * angle[:, None]) % NA * (2.0 * np.pi / NA)
    cos, sin = np.cos(phase), np.sin(phase)
    forward = np.zeros((TABLE, 2 * LANES))
    for part in range(2):
        rows = slice(TOPPAD + part * NA, TOPPAD + part * NA + NA)
        re = slice(part * HALF, part * HALF + FREQS)
        im = slice(LANES + part * HALF, LANES + part * HALF + FREQS)
        forward[rows, re], forward[rows, im] = cos, -sin
    lane = np.arange(SEND_W)
    source = np.where(lane < IMG_W, IMG_W + NA * (lane // PAIR) + lane % NA, lane) - 512
    spread = (np.arange(384)[:, None] == source[None, :]) & (lane < ROW_W)[None, :]
    return split3(forward), spread.astype(bf16)


def dot(a, b):
    return lax.dot_general(a, b, (((1,), (0,)), ((), ())), preferred_element_type=f32)


def dot_t(a, b):
    return lax.dot_general(a, b, (((1,), (1,)), ((), ())), preferred_element_type=f32)


def dot_exact(a, b):
    return lax.dot_general(
        a,
        b,
        (((1,), (0,)), ((), ())),
        precision=lax.Precision.HIGHEST,
        preferred_element_type=f32,
    )


def window(table, block, index):
    start = TOPPAD - 16 * index
    return table[block, start : start + 2 * LANES, :]


def lanes_of(x, index):
    return x[:, LANES * index : LANES * index + 2 * LANES]


def lane_index(shape):
    return lax.broadcasted_iota(jnp.int32, shape, len(shape) - 1)


def inverse_weights():
    freq = lane_index((1, LANES)) % HALF
    ends = (freq == 0) | (freq == NA // 2)
    return jnp.where(freq < FREQS, jnp.where(ends, 1.0 / NA, 2.0 / NA), 0.0).astype(f32)


def rows_summed(tiles):
    line = lax.broadcasted_iota(jnp.int32, (8, LANES), 0)
    for k in (1, 2, 4):
        mine = (line & k) == 0
        tiles = [
            jnp.where(mine, a, b) + pltpu.roll(jnp.where(mine, b, a), 8 - k, 0)
            for a, b in zip(tiles[::2], tiles[1::2])
        ]
    return tiles[0]


def forward_wave(x, table, index, splits=3):
    return sum(dot(x, window(table, k, index)) for k in range(splits))


def pack_kernel(images, ctf, classes, place, wsend):
    width = SEND_W - ROW_W
    lookup = place[...].astype(f32).astype(bf16)
    line = lax.broadcasted_iota(jnp.int32, (16, 16), 0)
    listed = jnp.zeros((16, 16), f32)
    for j in range(TOP):
        hit = classes[j : j + 1, :] == lax.broadcasted_iota(jnp.int32, (place.shape[1], 16), 0)
        row = dot(lookup, jnp.where(hit, 1.0, 0.0).astype(bf16))
        listed = jnp.where(line == j, row, listed)
    tail = jnp.concatenate([listed, jnp.zeros((16, width - 16), f32)], axis=1).astype(bf16)
    for h in range(2):
        for i in range(8):
            shell = i * 8 + h * SHELLS
            wsend[h * 8 + i] = jnp.concatenate(
                [
                    images[:, shell * PAIR : shell * PAIR + IMG_W],
                    ctf[:, shell * NA : shell * NA + CTF_W],
                    tail,
                ],
                axis=1,
            )


def copies_kernel(at, refs, rsend):
    start = pl.multiple_of(at[0] * 2 * IMG_W, LANES)
    mine = refs[:, pl.ds(start, 2 * IMG_W)].astype(f32)
    for h in range(2):
        half = mine[:, h * IMG_W : (h + 1) * IMG_W]
        half = jnp.concatenate([half, jnp.zeros((7, REF_W - IMG_W), f32)], axis=1)
        half = jnp.concatenate([half, jnp.zeros((1, REF_W), f32)], axis=0).astype(bf16)
        for o in range(OWNERS):
            if (o // 8) % 2 == h:
                rsend[o] = half


def weigh_kernel(recv, inv, spread, table, wre, wim):
    scale = dot(recv[:, 512:], spread[...]) * inv[...]
    weighted = (recv[...].astype(f32) * scale).astype(bf16)
    for s in range(WINDOWS):
        y = forward_wave(lanes_of(weighted, s), table, s)
        wre[pl.ds(s, PARTICLES, stride=PITCH), :] = y[:, :LANES]
        wim[pl.ds(s, PARTICLES, stride=PITCH), :] = y[:, LANES:]
    zero = jnp.zeros((PARTICLES, LANES), f32)
    for s in range(WINDOWS, PITCH):
        wre[pl.ds(s, PARTICLES, stride=PITCH), :] = zero
        wim[pl.ds(s, PARTICLES, stride=PITCH), :] = zero


def score_kernel(idx, recv, table, wre, wim, out, rre, rim, pq):
    raw32 = recv[...].astype(f32).reshape(TABLE_ROWS, REF_W)
    raw = raw32.astype(bf16)
    square = raw32 * raw32
    left = square + jnp.concatenate([square[:, NA:], square[:, :NA]], axis=1)
    right = square + jnp.concatenate([square[:, REF_W - NA :], square[:, : REF_W - NA]], axis=1)
    lane = lane_index((1, REF_W))
    even = (lane < NA) | ((lane >= 2 * PAIR) & (lane < 2 * PAIR + NA))
    odd = ((lane >= PAIR + NA) & (lane < 2 * PAIR)) | (
        (lane >= 3 * PAIR + NA) & (lane < 4 * PAIR)
    )
    power = jnp.where(even, left, jnp.where(odd, right, 0.0)).astype(bf16).astype(f32)
    power = (-0.5 * power).astype(bf16)
    for s in range(SHELLS):
        y = forward_wave(lanes_of(raw, s), table, s)
        rre[pl.ds(s, TABLE_ROWS, stride=PITCH), :] = y[:, :LANES]
        rim[pl.ds(s, TABLE_ROWS, stride=PITCH), :] = y[:, LANES:]
    for j in range(SHELLS // 2):
        y = sum(forward_wave(lanes_of(power, s), table, s) for s in (2 * j, 2 * j + 1))
        rre[pl.ds(SHELLS + j, TABLE_ROWS, stride=PITCH), :] = y[:, :LANES]
        rim[pl.ds(SHELLS + j, TABLE_ROWS, stride=PITCH), :] = y[:, LANES:]
    zero = jnp.zeros((TABLE_ROWS, LANES), f32)
    for s in range(WINDOWS, PITCH):
        rre[pl.ds(s, TABLE_ROWS, stride=PITCH), :] = zero
        rim[pl.ds(s, TABLE_ROWS, stride=PITCH), :] = zero

    def block(b, carry):
        rows = [[[], []] for _ in range(TOP)]
        for u in range(8):
            i = b * 8 + u
            at = pl.multiple_of(i * PITCH, PITCH)
            a_re = wre[pl.ds(at, PITCH), :]
            a_im = wim[pl.ds(at, PITCH), :]
            for j in range(TOP):
                t = pl.multiple_of(idx[b // 2 * 64 + j * 16 + b % 2 * 8 + u] * PITCH, PITCH)
                b_re = rre[pl.ds(t, PITCH), :]
                b_im = rim[pl.ds(t, PITCH), :]
                p = a_re * b_re + a_im * b_im
                q = a_im * b_re - a_re * b_im
                rows[j][0].append(p)
                rows[j][1].append(q)
        at = pl.multiple_of(b * 8, 8)
        for j in range(TOP):
            pq[j, pl.ds(at, 8), :LANES] = rows_summed(rows[j][0])
            pq[j, pl.ds(at, 8), LANES:] = rows_summed(rows[j][1])
        return carry

    lax.fori_loop(0, PARTICLES // 8, block, 0)
    weights = inverse_weights()
    low = lane_index((1, LANES)) < HALF
    windows = []
    for j in range(0, TOP, 2):
        sides = []
        for at in (0, LANES):
            first, second = pq[j, :, at : at + LANES], pq[j + 1, :, at : at + LANES]
            first = first + pltpu.roll(first, HALF, 1)
            second = second + pltpu.roll(second, HALF, 1)
            sides.append(jnp.where(low, first, second) * weights)
        x = jnp.concatenate(sides, axis=1)
        hi = x.astype(bf16)
        rest = x - hi.astype(f32)
        mid = rest.astype(bf16)
        small = (rest - mid.astype(f32)).astype(bf16)
        t = [window(table, k, j // 2) for k in range(3)]
        y = dot_t(small, t[0]) + dot_t(hi, t[2]) + dot_t(mid, t[1])
        y = y + (dot_t(mid, t[0]) + dot_t(hi, t[1]))
        windows.append(y + dot_t(hi, t[0]))
    out[:, :LANES] = windows[0][:, :LANES]
    out[:, LANES : 2 * LANES] = windows[0][:, LANES:] + windows[1][:, :LANES]
    out[:, 2 * LANES :] = windows[1][:, LANES:]


def softmax_kernel(parts, out):
    logits = parts[0]
    for k in range(1, MEMBERS):
        logits += parts[k]
    logits = jnp.where(lane_index(logits.shape) < TOP * NA, logits, -jnp.inf)
    highest = jnp.max(logits, axis=1, keepdims=True)
    e = jnp.exp(logits - highest)
    posterior = (e / jnp.sum(e, axis=1, keepdims=True)).astype(bf16)
    for k in range(MEMBERS):
        out[k] = posterior


def gather_kernel(idx, post, table, wre, wim, out, gre, gim, are, aim):
    lane = lane_index((1, 2 * LANES))
    for j in range(TOP):
        first = 16 * (j // 2) + NA * (j % 2)
        mine = (lane >= first) & (lane < first + NA)
        x = jnp.where(mine, lanes_of(post[...].astype(f32), j // 2), 0.0).astype(bf16)
        y = forward_wave(x, table, j // 2, splits=2)
        gre[j] = y[:, :LANES] + pltpu.roll(y[:, :LANES], HALF, 1)
        gim[j] = y[:, LANES:] + pltpu.roll(y[:, LANES:], HALF, 1)
    are[...] = jnp.zeros_like(are)
    aim[...] = jnp.zeros_like(aim)

    def block(b, carry):
        for u in range(4):
            i = b * 4 + u
            at = pl.multiple_of(i * PITCH, PITCH)
            a_re = wre[pl.ds(at, PITCH), :]
            a_im = wim[pl.ds(at, PITCH), :]
            pending = []
            for j in range(TOP):
                where = b // 4 * 64 + j * 16 + b % 4 * 4 + u
                t = pl.multiple_of(idx[where] * PITCH, PITCH)
                g_re = gre[j, pl.ds(i, 1), :]
                g_im = gim[j, pl.ds(i, 1), :]
                pending.append((are, t, are[pl.ds(t, PITCH), :] + (a_re * g_re + a_im * g_im)))
                pending.append((aim, t, aim[pl.ds(t, PITCH), :] + (a_im * g_re - a_re * g_im)))
            for ref, t, value in pending:
                ref[pl.ds(t, PITCH), :] = value
        return carry

    lax.fori_loop(0, PARTICLES // 4, block, 0)
    weights = inverse_weights()
    before = None
    for s in range(WINDOWS):
        lines = pl.ds(s, TABLE_ROWS, stride=PITCH)
        x = jnp.concatenate(
            [are[lines, :] * weights, aim[lines, :] * weights], axis=1
        )
        hi = x.astype(bf16)
        low = (x - hi.astype(f32)).astype(bf16)
        t_hi, t_low = window(table, 0, s), window(table, 1, s)
        y = dot_t(hi, t_hi) + dot_t(low, t_hi) + dot_t(hi, t_low)
        tile = y[:, :LANES] if before is None else before + y[:, :LANES]
        out[:, :, LANES * s : LANES * s + LANES] = tile.reshape(OWNERS, 8, LANES).astype(bf16)
        before = y[:, LANES:]
    out[:, :, LANES * WINDOWS :] = before.reshape(OWNERS, 8, LANES).astype(bf16)


def final_kernel(parts, spread, out):
    sums = []
    for h in range(2):
        members = [s for s in range(OWNERS) if (s // 8) % 2 == h]
        total = parts[members[0]].astype(f32)
        for s in members[1:]:
            total += parts[s].astype(f32)
        sums.append(total)
    total = jnp.concatenate(sums, axis=0)
    under = dot_exact(total[:, 512:] + 1.0, spread[:, :REF_W].astype(f32))[:, :IMG_W]
    new = total[:, :IMG_W] / under
    out[:, :IMG_W] = new[:7]
    out[:, IMG_W:] = new[8:15]


VM = pl.BlockSpec(memory_space=pltpu.VMEM)
SM = pl.BlockSpec(memory_space=pltpu.SMEM)


def call(kernel, name, out_shape, in_specs, args, scratch=(), limit=24):
    out_specs = tuple(VM for _ in out_shape) if isinstance(out_shape, tuple) else VM
    return pl.pallas_call(
        kernel,
        out_shape=out_shape,
        in_specs=in_specs,
        out_specs=out_specs,
        scratch_shapes=scratch,
        compiler_params=pltpu.CompilerParams(vmem_limit_bytes=limit * 1024 * 1024),
        name=name,
    )(*args)


def on_device(images, ctf, classes, class_place, references, sigma2):
    table, spread = make_tables()
    img, h = lax.axis_index("img"), lax.axis_index("xl")
    shape = jax.ShapeDtypeStruct
    wsend = call(
        pack_kernel,
        "pack",
        shape((MEMBERS, 16, SEND_W), bf16),
        [VM] * 4,
        (images, ctf, classes.T, class_place.reshape(1, -1)),
        limit=58,
    )
    rsend = call(
        copies_kernel,
        "copies",
        shape((OWNERS, 8, REF_W), bf16),
        [SM, VM],
        (img.reshape(1), references),
        limit=8,
    )
    wrecv = lax.all_to_all(wsend, GROUP, 0, 0, tiled=True)
    rrecv = lax.all_to_all(rsend, CLS, 0, 0, tiled=True)
    listed = wrecv[:, :TOP, ROW_W : ROW_W + 16].astype(jnp.int32)
    idx = (listed // 7 * 8 + listed % 7).reshape(-1)
    wrecv = wrecv.reshape(PARTICLES, SEND_W)
    inv = 1.0 / lax.dynamic_slice(sigma2, (img * 8 + h * SHELLS,), (SHELLS,))
    inv = jnp.concatenate(
        [jnp.repeat(inv, PAIR), jnp.repeat(inv, NA), jnp.zeros((SEND_W - ROW_W,), f32)]
    ).reshape(1, SEND_W)
    hat = shape((PARTICLES * PITCH, LANES), f32)
    wre, wim = call(
        weigh_kernel, "weigh", (hat, hat), [VM] * 4, (wrecv, inv, spread, table)
    )
    rows = pltpu.VMEM((TABLE_ROWS * PITCH, LANES), f32)
    partial = call(
        score_kernel,
        "score",
        shape((PARTICLES, LOGIT_W), f32),
        [SM] + [VM] * 4,
        (idx, rrecv, table, wre, wim),
        [rows, rows, pltpu.VMEM((TOP, PARTICLES, 2 * LANES), f32)],
    )
    parts = lax.all_to_all(partial.reshape(MEMBERS, 16, LOGIT_W), GROUP, 0, 0, tiled=True)
    post = call(
        softmax_kernel, "softmax", shape((MEMBERS, 16, LOGIT_W), bf16), [VM], (parts,)
    )
    post = lax.all_to_all(post, GROUP, 0, 0, tiled=True).reshape(PARTICLES, LOGIT_W)
    each = pltpu.VMEM((TOP, PARTICLES, LANES), f32)
    sums = call(
        gather_kernel,
        "gather",
        shape((OWNERS, 8, SEND_W), bf16),
        [SM] + [VM] * 4,
        (idx, post, table, wre, wim),
        [each, each, rows, rows],
    )
    arrived = lax.all_to_all(sums, CLS, 0, 0, tiled=True)
    return call(
        final_kernel, "final", shape((7, 2 * IMG_W), f32), [VM, VM], (arrived, spread)
    )


def solution(mesh):
    finer = Mesh(mesh.devices.reshape(2, 2, 8, 8), DEVICES)
    in_specs = (
        P(DEVICES, None),
        P(DEVICES, None),
        P(DEVICES, None),
        P(),
        P(CLS, None),
        P(),
    )
    return jax.shard_map(
        on_device, mesh=finer, in_specs=in_specs, out_specs=P(CLS, "img"), check_vma=False
    )
```

```python
import jax
import jax.numpy as jnp
import numpy as np
from jax import lax
from jax.experimental import pallas as pl
from jax.experimental.pallas import tpu as pltpu
from jax.sharding import Mesh
from jax.sharding import PartitionSpec as P

TOP = 4
NA = 72
HALF = 64
LANES = 128
PITCH = 16
SHELLS = 4
WINDOWS = 6
MEMBERS = 16
PARTICLES = 16 * MEMBERS
OWNERS = 32
TABLE_ROWS = 8 * OWNERS
PAIR = 2 * NA
IMG_W = SHELLS * PAIR
CTF_W = SHELLS * NA
REF_W = 640
ROW_W = IMG_W + CTF_W
SEND_W = 896
LOGIT_W = 384
FREQS = NA // 2 + 1
TOPPAD = 112
TABLE = 384
CLS = ("x", "zh", "zl")
GROUP = ("zl", "img")
DEVICES = ("x", "zh", "zl", "img")

bf16 = jnp.bfloat16
f32 = jnp.float32


def split3(x):
    x = np.asarray(x, np.float32)
    hi = x.astype(bf16)
    rest = x - hi.astype(np.float32)
    mid = rest.astype(bf16)
    low = (rest - mid.astype(np.float32)).astype(bf16)
    return np.stack([hi, mid, low])


def make_tables():
    freq = np.arange(FREQS)
    angle = np.arange(NA)
    phase = (freq[None, :] * angle[:, None]) % NA * (2.0 * np.pi / NA)
    cos, sin = np.cos(phase), np.sin(phase)
    forward = np.zeros((TABLE, 2 * LANES))
    for part in range(2):
        rows = slice(TOPPAD + part * NA, TOPPAD + part * NA + NA)
        re = slice(part * HALF, part * HALF + FREQS)
        im = slice(LANES + part * HALF, LANES + part * HALF + FREQS)
        forward[rows, re], forward[rows, im] = cos, -sin
    lane = np.arange(SEND_W)
    source = np.where(lane < IMG_W, IMG_W + NA * (lane // PAIR) + lane % NA, lane) - 512
    spread = (np.arange(384)[:, None] == source[None, :]) & (lane < ROW_W)[None, :]
    return split3(forward), spread.astype(bf16)


def dot(a, b):
    return lax.dot_general(a, b, (((1,), (0,)), ((), ())), preferred_element_type=f32)


def dot_t(a, b):
    return lax.dot_general(a, b, (((1,), (1,)), ((), ())), preferred_element_type=f32)


def dot_exact(a, b):
    return lax.dot_general(
        a,
        b,
        (((1,), (0,)), ((), ())),
        precision=lax.Precision.HIGHEST,
        preferred_element_type=f32,
    )


def window(table, block, index):
    start = TOPPAD - 16 * index
    return table[block, start : start + 2 * LANES, :]


def lanes_of(x, index):
    return x[:, LANES * index : LANES * index + 2 * LANES]


def lane_index(shape):
    return lax.broadcasted_iota(jnp.int32, shape, len(shape) - 1)


def inverse_weights():
    freq = lane_index((1, LANES)) % HALF
    ends = (freq == 0) | (freq == NA // 2)
    return jnp.where(freq < FREQS, jnp.where(ends, 1.0 / NA, 2.0 / NA), 0.0).astype(f32)


def put(hat, count, s, y):
    hat[pl.ds(s, count, stride=PITCH), :] = y[:, :LANES]
    hat[pl.ds(8 + s, count, stride=PITCH), :] = y[:, LANES:]


def clear_rest(hat, count):
    zero = jnp.zeros((count, LANES), f32)
    for s in range(WINDOWS, 8):
        hat[pl.ds(s, count, stride=PITCH), :] = zero
        hat[pl.ds(8 + s, count, stride=PITCH), :] = zero


def rows_summed(tiles):
    line = lax.broadcasted_iota(jnp.int32, (8, LANES), 0)
    for k in (1, 2, 4):
        mine = (line & k) == 0
        tiles = [
            jnp.where(mine, a, b) + pltpu.roll(jnp.where(mine, b, a), 8 - k, 0)
            for a, b in zip(tiles[::2], tiles[1::2])
        ]
    return tiles[0]


def forward_wave(x, table, index, splits=3):
    return sum(dot(x, window(table, k, index)) for k in range(splits))


def pack_kernel(images, ctf, classes, place, wsend):
    width = SEND_W - ROW_W
    lookup = place[...].astype(f32).astype(bf16)
    line = lax.broadcasted_iota(jnp.int32, (16, 16), 0)
    listed = jnp.zeros((16, 16), f32)
    for j in range(TOP):
        hit = classes[j : j + 1, :] == lax.broadcasted_iota(jnp.int32, (place.shape[1], 16), 0)
        row = dot(lookup, jnp.where(hit, 1.0, 0.0).astype(bf16))
        listed = jnp.where(line == j, row, listed)
    tail = jnp.concatenate([listed, jnp.zeros((16, width - 16), f32)], axis=1).astype(bf16)
    for h in range(2):
        for i in range(8):
            shell = i * 8 + h * SHELLS
            wsend[h * 8 + i] = jnp.concatenate(
                [
                    images[:, shell * PAIR : shell * PAIR + IMG_W],
                    ctf[:, shell * NA : shell * NA + CTF_W],
                    tail,
                ],
                axis=1,
            )


def copies_kernel(at, refs, rsend):
    start = pl.multiple_of(at[0] * 2 * IMG_W, LANES)
    mine = refs[:, pl.ds(start, 2 * IMG_W)].astype(f32)
    for h in range(2):
        half = mine[:, h * IMG_W : (h + 1) * IMG_W]
        half = jnp.concatenate([half, jnp.zeros((7, REF_W - IMG_W), f32)], axis=1)
        half = jnp.concatenate([half, jnp.zeros((1, REF_W), f32)], axis=0).astype(bf16)
        for o in range(OWNERS):
            if o % 2 == h:
                rsend[o] = half


def weigh_kernel(recv, inv, spread, table, hat):
    scale = dot(recv[:, 512:], spread[...]) * inv[...]
    weighted = (recv[...].astype(f32) * scale).astype(bf16)
    for s in range(WINDOWS):
        y = forward_wave(lanes_of(weighted, s), table, s)
        put(hat, PARTICLES, s, y)
    clear_rest(hat, PARTICLES)


def score_kernel(idx, recv, table, what, out, rhat, pq):
    raw32 = recv[...].astype(f32).reshape(TABLE_ROWS, REF_W)
    raw = raw32.astype(bf16)
    square = raw32 * raw32
    left = square + jnp.concatenate([square[:, NA:], square[:, :NA]], axis=1)
    right = square + jnp.concatenate([square[:, REF_W - NA :], square[:, : REF_W - NA]], axis=1)
    lane = lane_index((1, REF_W))
    even = (lane < NA) | ((lane >= 2 * PAIR) & (lane < 2 * PAIR + NA))
    odd = ((lane >= PAIR + NA) & (lane < 2 * PAIR)) | (
        (lane >= 3 * PAIR + NA) & (lane < 4 * PAIR)
    )
    power = jnp.where(even, left, jnp.where(odd, right, 0.0)).astype(bf16).astype(f32)
    power = (-0.5 * power).astype(bf16)
    for s in range(SHELLS):
        put(rhat, TABLE_ROWS, s, forward_wave(lanes_of(raw, s), table, s))
    for j in range(SHELLS // 2):
        y = sum(forward_wave(lanes_of(power, s), table, s) for s in (2 * j, 2 * j + 1))
        put(rhat, TABLE_ROWS, SHELLS + j, y)
    clear_rest(rhat, TABLE_ROWS)

    def block(b, carry):
        rows = [[[], []] for _ in range(TOP)]
        first = b // 2 * 64 + b % 2 * 8
        for u in range(8):
            at = pl.multiple_of((b * 8 + u) * PITCH, PITCH)
            a_re = what[pl.ds(at, 8), :]
            a_im = what[pl.ds(at + 8, 8), :]
            for j in range(TOP):
                t = pl.multiple_of(idx[first + (j * 16 + u)], PITCH)
                b_re = rhat[pl.ds(t, 8), :]
                b_im = rhat[pl.ds(t + 8, 8), :]
                p = a_re * b_re + a_im * b_im
                q = a_im * b_re - a_re * b_im
                rows[j][0].append(p)
                rows[j][1].append(q)
        at = pl.multiple_of(b * 8, 8)
        for j in range(TOP):
            pq[j, pl.ds(at, 8), :LANES] = rows_summed(rows[j][0])
            pq[j, pl.ds(at, 8), LANES:] = rows_summed(rows[j][1])
        return carry

    lax.fori_loop(0, PARTICLES // 8, block, 0, unroll=4)
    weights = inverse_weights()
    low = lane_index((1, LANES)) < HALF
    windows = []
    for j in range(0, TOP, 2):
        sides = []
        for at in (0, LANES):
            first, second = pq[j, :, at : at + LANES], pq[j + 1, :, at : at + LANES]
            first = first + pltpu.roll(first, HALF, 1)
            second = second + pltpu.roll(second, HALF, 1)
            sides.append(jnp.where(low, first, second) * weights)
        x = jnp.concatenate(sides, axis=1)
        hi = x.astype(bf16)
        rest = x - hi.astype(f32)
        mid = rest.astype(bf16)
        small = (rest - mid.astype(f32)).astype(bf16)
        t = [window(table, k, j // 2) for k in range(3)]
        y = dot_t(small, t[0]) + dot_t(hi, t[2]) + dot_t(mid, t[1])
        y = y + (dot_t(mid, t[0]) + dot_t(hi, t[1]))
        windows.append(y + dot_t(hi, t[0]))
    out[:, :LANES] = windows[0][:, :LANES]
    out[:, LANES : 2 * LANES] = windows[0][:, LANES:] + windows[1][:, :LANES]
    out[:, 2 * LANES :] = windows[1][:, LANES:]


def softmax_kernel(parts, out):
    logits = parts[0]
    for k in range(1, MEMBERS):
        logits += parts[k]
    logits = jnp.where(lane_index(logits.shape) < TOP * NA, logits, -jnp.inf)
    highest = jnp.max(logits, axis=1, keepdims=True)
    e = jnp.exp(logits - highest)
    posterior = (e / jnp.sum(e, axis=1, keepdims=True)).astype(bf16)
    for k in range(MEMBERS):
        out[k] = posterior


def gather_kernel(idx, post, table, what, out, waves, total):
    lane = lane_index((1, 2 * LANES))
    for j in range(TOP):
        first = 16 * (j // 2) + NA * (j % 2)
        mine = (lane >= first) & (lane < first + NA)
        x = jnp.where(mine, lanes_of(post[...].astype(f32), j // 2), 0.0).astype(bf16)
        y = forward_wave(x, table, j // 2, splits=2)
        waves[2 * j] = y[:, :LANES] + pltpu.roll(y[:, :LANES], HALF, 1)
        waves[2 * j + 1] = y[:, LANES:] + pltpu.roll(y[:, LANES:], HALF, 1)
    total[...] = jnp.zeros_like(total)

    def block(b, carry):
        first = b // 2 * 64 + b % 2 * 8
        lines = pl.ds(pl.multiple_of(b * 8, 8), 8)
        tiles = [waves[k, lines, :] for k in range(2 * TOP)]
        for u in range(8):
            at = pl.multiple_of((b * 8 + u) * PITCH, PITCH)
            a_re = what[pl.ds(at, 8), :]
            a_im = what[pl.ds(at + 8, 8), :]
            pending = []
            for j in range(TOP):
                t = pl.multiple_of(idx[first + (j * 16 + u)], PITCH)
                g_re = tiles[2 * j][u : u + 1]
                g_im = tiles[2 * j + 1][u : u + 1]
                re = total[pl.ds(t, 8), :] + (a_re * g_re + a_im * g_im)
                im = total[pl.ds(t + 8, 8), :] + (a_im * g_re - a_re * g_im)
                pending.append((t, re, im))
            for t, re, im in pending:
                total[pl.ds(t, 8), :] = re
                total[pl.ds(t + 8, 8), :] = im
        return carry

    lax.fori_loop(0, PARTICLES // 8, block, 0)
    weights = inverse_weights()
    before = None
    for s in range(WINDOWS):
        x = jnp.concatenate(
            [total[pl.ds(8 * k + s, TABLE_ROWS, stride=PITCH), :] * weights for k in range(2)],
            axis=1,
        )
        hi = x.astype(bf16)
        low = (x - hi.astype(f32)).astype(bf16)
        t_hi, t_low = window(table, 0, s), window(table, 1, s)
        y = dot_t(hi, t_hi) + dot_t(low, t_hi) + dot_t(hi, t_low)
        tile = y[:, :LANES] if before is None else before + y[:, :LANES]
        out[:, :, LANES * s : LANES * s + LANES] = tile.reshape(OWNERS, 8, LANES).astype(bf16)
        before = y[:, LANES:]
    out[:, :, LANES * WINDOWS :] = before.reshape(OWNERS, 8, LANES).astype(bf16)


def final_kernel(parts, spread, out):
    sums = []
    for h in range(2):
        members = [s for s in range(OWNERS) if s % 2 == h]
        total = parts[members[0]].astype(f32)
        for s in members[1:]:
            total += parts[s].astype(f32)
        sums.append(total)
    total = jnp.concatenate(sums, axis=0)
    under = dot_exact(total[:, 512:] + 1.0, spread[:, :REF_W].astype(f32))[:, :IMG_W]
    new = total[:, :IMG_W] / under
    out[:, :IMG_W] = new[:7]
    out[:, IMG_W:] = new[8:15]


VM = pl.BlockSpec(memory_space=pltpu.VMEM)
SM = pl.BlockSpec(memory_space=pltpu.SMEM)


def call(kernel, name, out_shape, in_specs, args, scratch=(), limit=24):
    out_specs = tuple(VM for _ in out_shape) if isinstance(out_shape, tuple) else VM
    return pl.pallas_call(
        kernel,
        out_shape=out_shape,
        in_specs=in_specs,
        out_specs=out_specs,
        scratch_shapes=scratch,
        compiler_params=pltpu.CompilerParams(vmem_limit_bytes=limit * 1024 * 1024),
        name=name,
    )(*args)


def on_device(images, ctf, classes, class_place, references, sigma2):
    table, spread = make_tables()
    img, h = lax.axis_index("img"), lax.axis_index("zl")
    shape = jax.ShapeDtypeStruct
    wsend = call(
        pack_kernel,
        "pack",
        shape((MEMBERS, 16, SEND_W), bf16),
        [VM] * 4,
        (images, ctf, classes.T, class_place.reshape(1, -1)),
        limit=58,
    )
    rsend = call(
        copies_kernel,
        "copies",
        shape((OWNERS, 8, REF_W), bf16),
        [SM, VM],
        (img.reshape(1), references),
        limit=8,
    )
    wrecv = lax.all_to_all(wsend, GROUP, 0, 0, tiled=True)
    rrecv = lax.all_to_all(rsend, CLS, 0, 0, tiled=True)
    listed = wrecv[:, :TOP, ROW_W : ROW_W + 16].astype(jnp.int32)
    idx = ((listed // 7 * 8 + listed % 7) * PITCH).reshape(-1)
    wrecv = wrecv.reshape(PARTICLES, SEND_W)
    inv = 1.0 / lax.dynamic_slice(sigma2, (img * 8 + h * SHELLS,), (SHELLS,))
    inv = jnp.concatenate(
        [jnp.repeat(inv, PAIR), jnp.repeat(inv, NA), jnp.zeros((SEND_W - ROW_W,), f32)]
    ).reshape(1, SEND_W)
    hat = shape((PARTICLES * PITCH, LANES), f32)
    what = call(
        weigh_kernel, "weigh", hat, [VM] * 4, (wrecv, inv, spread, table)
    )
    rows = pltpu.VMEM((TABLE_ROWS * PITCH, LANES), f32)
    partial = call(
        score_kernel,
        "score",
        shape((PARTICLES, LOGIT_W), f32),
        [SM] + [VM] * 3,
        (idx, rrecv, table, what),
        [rows, pltpu.VMEM((TOP, PARTICLES, 2 * LANES), f32)],
    )
    parts = lax.all_to_all(partial.reshape(MEMBERS, 16, LOGIT_W), GROUP, 0, 0, tiled=True)
    post = call(
        softmax_kernel, "softmax", shape((MEMBERS, 16, LOGIT_W), bf16), [VM], (parts,)
    )
    post = lax.all_to_all(post, GROUP, 0, 0, tiled=True).reshape(PARTICLES, LOGIT_W)
    waves = pltpu.VMEM((2 * TOP, PARTICLES, LANES), f32)
    sums = call(
        gather_kernel,
        "gather",
        shape((OWNERS, 8, SEND_W), bf16),
        [SM] + [VM] * 3,
        (idx, post, table, what),
        [waves, rows],
    )
    arrived = lax.all_to_all(sums, CLS, 0, 0, tiled=True)
    return call(
        final_kernel, "final", shape((7, 2 * IMG_W), f32), [VM, VM], (arrived, spread)
    )


def solution(mesh):
    finer = Mesh(mesh.devices.reshape(4, 4, 2, 8), DEVICES)
    in_specs = (
        P(DEVICES, None),
        P(DEVICES, None),
        P(DEVICES, None),
        P(),
        P(CLS, None),
        P(),
    )
    return jax.shard_map(
        on_device, mesh=finer, in_specs=in_specs, out_specs=P(CLS, "img"), check_vma=False
    )
```

```python
import jax
import jax.numpy as jnp
import numpy as np
from jax import lax
from jax.experimental import pallas as pl
from jax.experimental.pallas import tpu as pltpu
from jax.sharding import Mesh
from jax.sharding import PartitionSpec as P

TOP = 4
NA = 72
HALF = 64
LANES = 128
PITCH = 16
SHELLS = 4
WINDOWS = 6
MEMBERS = 16
PARTICLES = 16 * MEMBERS
OWNERS = 32
TABLE_ROWS = 8 * OWNERS
PAIR = 2 * NA
IMG_W = SHELLS * PAIR
CTF_W = SHELLS * NA
REF_W = 640
ROW_W = IMG_W + CTF_W
SEND_W = 896
LOGIT_W = 384
FREQS = NA // 2 + 1
TOPPAD = 112
TABLE = 384
UNROLL = 4
CLS = ("x", "zh", "zl")
GROUP = ("zl", "img")
DEVICES = ("x", "zh", "zl", "img")

bf16 = jnp.bfloat16
f32 = jnp.float32


def split3(x):
    x = np.asarray(x, np.float32)
    hi = x.astype(bf16)
    rest = x - hi.astype(np.float32)
    mid = rest.astype(bf16)
    low = (rest - mid.astype(np.float32)).astype(bf16)
    return np.stack([hi, mid, low])


def make_tables():
    freq = np.arange(FREQS)
    angle = np.arange(NA)
    phase = (freq[None, :] * angle[:, None]) % NA * (2.0 * np.pi / NA)
    cos, sin = np.cos(phase), np.sin(phase)
    forward = np.zeros((TABLE, 2 * LANES))
    for part in range(2):
        rows = slice(TOPPAD + part * NA, TOPPAD + part * NA + NA)
        re = slice(part * HALF, part * HALF + FREQS)
        im = slice(LANES + part * HALF, LANES + part * HALF + FREQS)
        forward[rows, re], forward[rows, im] = cos, -sin
    lane = np.arange(SEND_W)
    source = np.where(lane < IMG_W, IMG_W + NA * (lane // PAIR) + lane % NA, lane) - 512
    spread = (np.arange(384)[:, None] == source[None, :]) & (lane < ROW_W)[None, :]
    return split3(forward), spread.astype(bf16)


def dot(a, b):
    return lax.dot_general(a, b, (((1,), (0,)), ((), ())), preferred_element_type=f32)


def dot_t(a, b):
    return lax.dot_general(a, b, (((1,), (1,)), ((), ())), preferred_element_type=f32)


def dot_exact(a, b):
    return lax.dot_general(
        a,
        b,
        (((1,), (0,)), ((), ())),
        precision=lax.Precision.HIGHEST,
        preferred_element_type=f32,
    )


def window(table, block, index):
    start = TOPPAD - 16 * index
    return table[block, start : start + 2 * LANES, :]


def lanes_of(x, index):
    return x[:, LANES * index : LANES * index + 2 * LANES]


def lane_index(shape):
    return lax.broadcasted_iota(jnp.int32, shape, len(shape) - 1)


def inverse_weights():
    freq = lane_index((1, LANES)) % HALF
    ends = (freq == 0) | (freq == NA // 2)
    return jnp.where(freq < FREQS, jnp.where(ends, 1.0 / NA, 2.0 / NA), 0.0).astype(f32)


def put(hat, count, s, y):
    hat[pl.ds(s, count, stride=PITCH), :] = y[:, :LANES]
    hat[pl.ds(8 + s, count, stride=PITCH), :] = y[:, LANES:]


def clear_rest(hat, count):
    zero = jnp.zeros((count, LANES), f32)
    for s in range(WINDOWS, 8):
        hat[pl.ds(s, count, stride=PITCH), :] = zero
        hat[pl.ds(8 + s, count, stride=PITCH), :] = zero


def rows_summed(tiles):
    line = lax.broadcasted_iota(jnp.int32, (8, LANES), 0)
    for k in (1, 2, 4):
        mine = (line & k) == 0
        tiles = [
            jnp.where(mine, a, b) + pltpu.roll(jnp.where(mine, b, a), 8 - k, 0)
            for a, b in zip(tiles[::2], tiles[1::2])
        ]
    return tiles[0]


def forward_wave(x, table, index, splits=3):
    return sum(dot(x, window(table, k, index)) for k in range(splits))


def pack_kernel(images, ctf, classes, place, wsend):
    width = SEND_W - ROW_W
    lookup = place[...].astype(f32).astype(bf16)
    line = lax.broadcasted_iota(jnp.int32, (16, 16), 0)
    listed = jnp.zeros((16, 16), f32)
    for j in range(TOP):
        hit = classes[j : j + 1, :] == lax.broadcasted_iota(jnp.int32, (place.shape[1], 16), 0)
        row = dot(lookup, jnp.where(hit, 1.0, 0.0).astype(bf16))
        listed = jnp.where(line == j, row, listed)
    tail = jnp.concatenate([listed, jnp.zeros((16, width - 16), f32)], axis=1).astype(bf16)
    for h in range(2):
        for i in range(8):
            shell = i * 8 + h * SHELLS
            wsend[h * 8 + i] = jnp.concatenate(
                [
                    images[:, shell * PAIR : shell * PAIR + IMG_W],
                    ctf[:, shell * NA : shell * NA + CTF_W],
                    tail,
                ],
                axis=1,
            )


def copies_kernel(at, refs, rsend):
    start = pl.multiple_of(at[0] * 2 * IMG_W, LANES)
    mine = refs[:, pl.ds(start, 2 * IMG_W)].astype(f32)
    for h in range(2):
        half = mine[:, h * IMG_W : (h + 1) * IMG_W]
        half = jnp.concatenate([half, jnp.zeros((7, REF_W - IMG_W), f32)], axis=1)
        half = jnp.concatenate([half, jnp.zeros((1, REF_W), f32)], axis=0).astype(bf16)
        for o in range(OWNERS):
            if o % 2 == h:
                rsend[o] = half


def weigh_kernel(recv, inv, spread, table, hat):
    scale = dot(recv[:, 512:], spread[...]) * inv[...]
    weighted = (recv[...].astype(f32) * scale).astype(bf16)
    for s in range(WINDOWS):
        y = forward_wave(lanes_of(weighted, s), table, s)
        put(hat, PARTICLES, s, y)
    clear_rest(hat, PARTICLES)


def score_kernel(places, recv, table, what, out, rhat, pq, idx, sem):
    copy = pltpu.make_async_copy(places, idx, sem)
    copy.start()
    raw32 = recv[...].astype(f32).reshape(TABLE_ROWS, REF_W)
    raw = raw32.astype(bf16)
    square = raw32 * raw32
    left = square + jnp.concatenate([square[:, NA:], square[:, :NA]], axis=1)
    right = square + jnp.concatenate([square[:, REF_W - NA :], square[:, : REF_W - NA]], axis=1)
    lane = lane_index((1, REF_W))
    even = (lane < NA) | ((lane >= 2 * PAIR) & (lane < 2 * PAIR + NA))
    odd = ((lane >= PAIR + NA) & (lane < 2 * PAIR)) | (
        (lane >= 3 * PAIR + NA) & (lane < 4 * PAIR)
    )
    power = jnp.where(even, left, jnp.where(odd, right, 0.0)).astype(bf16).astype(f32)
    power = (-0.5 * power).astype(bf16)
    for s in range(SHELLS):
        put(rhat, TABLE_ROWS, s, forward_wave(lanes_of(raw, s), table, s))
    for j in range(SHELLS // 2):
        y = sum(forward_wave(lanes_of(power, s), table, s) for s in (2 * j, 2 * j + 1))
        put(rhat, TABLE_ROWS, SHELLS + j, y)
    clear_rest(rhat, TABLE_ROWS)

    def block(b, carry):
        first = b // 2 * 64 + b % 2 * 8
        lines = pl.ds(pl.multiple_of(b * 8, 8), 8)
        rows = []
        for u in range(8):
            at = pl.multiple_of((b * 8 + u) * PITCH, PITCH)
            rows.append((what[pl.ds(at, 8), :], what[pl.ds(at + 8, 8), :]))
        for j in range(TOP):
            p, q = [], []
            for u, (a_re, a_im) in enumerate(rows):
                t = pl.multiple_of(idx[first + (j * 16 + u)], PITCH)
                b_re = rhat[pl.ds(t, 8), :]
                b_im = rhat[pl.ds(t + 8, 8), :]
                p.append(a_re * b_re + a_im * b_im)
                q.append(a_im * b_re - a_re * b_im)
            pq[j, lines, :LANES] = rows_summed(p)
            pq[j, lines, LANES:] = rows_summed(q)
        return carry

    copy.wait()
    lax.fori_loop(0, PARTICLES // 8, block, 0, unroll=UNROLL)
    weights = inverse_weights()
    low = lane_index((1, LANES)) < HALF
    windows = []
    for j in range(0, TOP, 2):
        sides = []
        for at in (0, LANES):
            first, second = pq[j, :, at : at + LANES], pq[j + 1, :, at : at + LANES]
            first = first + pltpu.roll(first, HALF, 1)
            second = second + pltpu.roll(second, HALF, 1)
            sides.append(jnp.where(low, first, second) * weights)
        x = jnp.concatenate(sides, axis=1)
        hi = x.astype(bf16)
        rest = x - hi.astype(f32)
        mid = rest.astype(bf16)
        small = (rest - mid.astype(f32)).astype(bf16)
        t = [window(table, k, j // 2) for k in range(3)]
        y = dot_t(small, t[0]) + dot_t(hi, t[2]) + dot_t(mid, t[1])
        y = y + (dot_t(mid, t[0]) + dot_t(hi, t[1]))
        windows.append(y + dot_t(hi, t[0]))
    out[:, :LANES] = windows[0][:, :LANES]
    out[:, LANES : 2 * LANES] = windows[0][:, LANES:] + windows[1][:, :LANES]
    out[:, 2 * LANES :] = windows[1][:, LANES:]


def softmax_kernel(parts, out):
    logits = parts[0]
    for k in range(1, MEMBERS):
        logits += parts[k]
    logits = jnp.where(lane_index(logits.shape) < TOP * NA, logits, -jnp.inf)
    highest = jnp.max(logits, axis=1, keepdims=True)
    e = jnp.exp(logits - highest)
    posterior = (e / jnp.sum(e, axis=1, keepdims=True)).astype(bf16)
    for k in range(MEMBERS):
        out[k] = posterior


def gather_kernel(places, post, table, what, out, waves, total, idx, sem):
    copy = pltpu.make_async_copy(places, idx, sem)
    copy.start()
    lane = lane_index((1, 2 * LANES))
    for j in range(TOP):
        first = 16 * (j // 2) + NA * (j % 2)
        mine = (lane >= first) & (lane < first + NA)
        x = jnp.where(mine, lanes_of(post[...].astype(f32), j // 2), 0.0).astype(bf16)
        y = forward_wave(x, table, j // 2, splits=2)
        waves[2 * j] = y[:, :LANES] + pltpu.roll(y[:, :LANES], HALF, 1)
        waves[2 * j + 1] = y[:, LANES:] + pltpu.roll(y[:, LANES:], HALF, 1)
    total[...] = jnp.zeros_like(total)

    def block(b, carry):
        first = b // 2 * 64 + b % 2 * 8
        lines = pl.ds(pl.multiple_of(b * 8, 8), 8)
        tiles = [waves[k, lines, :] for k in range(2 * TOP)]
        for u in range(8):
            at = pl.multiple_of((b * 8 + u) * PITCH, PITCH)
            a_re = what[pl.ds(at, 8), :]
            a_im = what[pl.ds(at + 8, 8), :]
            pending = []
            for j in range(TOP):
                t = pl.multiple_of(idx[first + (j * 16 + u)], PITCH)
                g_re = tiles[2 * j][u : u + 1]
                g_im = tiles[2 * j + 1][u : u + 1]
                re = total[pl.ds(t, 8), :] + (a_re * g_re + a_im * g_im)
                im = total[pl.ds(t + 8, 8), :] + (a_im * g_re - a_re * g_im)
                pending.append((t, re, im))
            for t, re, im in pending:
                total[pl.ds(t, 8), :] = re
                total[pl.ds(t + 8, 8), :] = im
        return carry

    copy.wait()
    lax.fori_loop(0, PARTICLES // 8, block, 0)
    weights = inverse_weights()
    before = None
    for s in range(WINDOWS):
        x = jnp.concatenate(
            [total[pl.ds(8 * k + s, TABLE_ROWS, stride=PITCH), :] * weights for k in range(2)],
            axis=1,
        )
        hi = x.astype(bf16)
        low = (x - hi.astype(f32)).astype(bf16)
        t_hi, t_low = window(table, 0, s), window(table, 1, s)
        y = dot_t(hi, t_hi) + dot_t(low, t_hi) + dot_t(hi, t_low)
        tile = y[:, :LANES] if before is None else before + y[:, :LANES]
        out[:, :, LANES * s : LANES * s + LANES] = tile.reshape(OWNERS, 8, LANES).astype(bf16)
        before = y[:, LANES:]
    out[:, :, LANES * WINDOWS :] = before.reshape(OWNERS, 8, LANES).astype(bf16)


def final_kernel(parts, spread, out):
    sums = []
    for h in range(2):
        members = [s for s in range(OWNERS) if s % 2 == h]
        total = parts[members[0]].astype(f32)
        for s in members[1:]:
            total += parts[s].astype(f32)
        sums.append(total)
    total = jnp.concatenate(sums, axis=0)
    under = dot_exact(total[:, 512:] + 1.0, spread[:, :REF_W].astype(f32))[:, :IMG_W]
    new = total[:, :IMG_W] / under
    out[:, :IMG_W] = new[:7]
    out[:, IMG_W:] = new[8:15]


VM = pl.BlockSpec(memory_space=pltpu.VMEM)
SM = pl.BlockSpec(memory_space=pltpu.SMEM)
ANY = pl.BlockSpec(memory_space=pl.ANY)


def call(kernel, name, out_shape, in_specs, args, scratch=(), limit=24):
    out_specs = tuple(VM for _ in out_shape) if isinstance(out_shape, tuple) else VM
    return pl.pallas_call(
        kernel,
        out_shape=out_shape,
        in_specs=in_specs,
        out_specs=out_specs,
        scratch_shapes=scratch,
        compiler_params=pltpu.CompilerParams(vmem_limit_bytes=limit * 1024 * 1024),
        name=name,
    )(*args)


def on_device(images, ctf, classes, class_place, references, sigma2):
    table, spread = make_tables()
    img, h = lax.axis_index("img"), lax.axis_index("zl")
    shape = jax.ShapeDtypeStruct
    wsend = call(
        pack_kernel,
        "pack",
        shape((MEMBERS, 16, SEND_W), bf16),
        [VM] * 4,
        (images, ctf, classes.T, class_place.reshape(1, -1)),
        limit=58,
    )
    rsend = call(
        copies_kernel,
        "copies",
        shape((OWNERS, 8, REF_W), bf16),
        [SM, VM],
        (img.reshape(1), references),
        limit=8,
    )
    wrecv = lax.all_to_all(wsend, GROUP, 0, 0, tiled=True)
    rrecv = lax.all_to_all(rsend, CLS, 0, 0, tiled=True)
    listed = wrecv[:, :TOP, ROW_W : ROW_W + 16].astype(jnp.int32)
    idx = ((listed // 7 * 8 + listed % 7) * PITCH).reshape(-1)
    wrecv = wrecv.reshape(PARTICLES, SEND_W)
    inv = 1.0 / lax.dynamic_slice(sigma2, (img * 8 + h * SHELLS,), (SHELLS,))
    inv = jnp.concatenate(
        [jnp.repeat(inv, PAIR), jnp.repeat(inv, NA), jnp.zeros((SEND_W - ROW_W,), f32)]
    ).reshape(1, SEND_W)
    hat = shape((PARTICLES * PITCH, LANES), f32)
    what = call(
        weigh_kernel, "weigh", hat, [VM] * 4, (wrecv, inv, spread, table)
    )
    rows = pltpu.VMEM((TABLE_ROWS * PITCH, LANES), f32)
    places = [pltpu.SMEM((PARTICLES * TOP,), jnp.int32), pltpu.SemaphoreType.DMA]
    partial = call(
        score_kernel,
        "score",
        shape((PARTICLES, LOGIT_W), f32),
        [ANY] + [VM] * 3,
        (idx, rrecv, table, what),
        [rows, pltpu.VMEM((TOP, PARTICLES, 2 * LANES), f32), *places],
    )
    parts = lax.all_to_all(partial.reshape(MEMBERS, 16, LOGIT_W), GROUP, 0, 0, tiled=True)
    post = call(
        softmax_kernel, "softmax", shape((MEMBERS, 16, LOGIT_W), bf16), [VM], (parts,)
    )
    post = lax.all_to_all(post, GROUP, 0, 0, tiled=True).reshape(PARTICLES, LOGIT_W)
    waves = pltpu.VMEM((2 * TOP, PARTICLES, LANES), f32)
    sums = call(
        gather_kernel,
        "gather",
        shape((OWNERS, 8, SEND_W), bf16),
        [ANY] + [VM] * 3,
        (idx, post, table, what),
        [waves, rows, *places],
    )
    arrived = lax.all_to_all(sums, CLS, 0, 0, tiled=True)
    return call(
        final_kernel, "final", shape((7, 2 * IMG_W), f32), [VM, VM], (arrived, spread)
    )


def solution(mesh):
    finer = Mesh(mesh.devices.reshape(4, 4, 2, 8), DEVICES)
    in_specs = (
        P(DEVICES, None),
        P(DEVICES, None),
        P(DEVICES, None),
        P(),
        P(CLS, None),
        P(),
    )
    return jax.shard_map(
        on_device, mesh=finer, in_specs=in_specs, out_specs=P(CLS, "img"), check_vma=False
    )
```

```python
import jax
import jax.numpy as jnp
import numpy as np
from jax import lax
from jax.experimental import pallas as pl
from jax.experimental.pallas import tpu as pltpu
from jax.sharding import Mesh
from jax.sharding import PartitionSpec as P

TOP = 4
NA = 72
HALF = 64
LANES = 128
PITCH = 16
SHELLS = 4
WINDOWS = 6
MEMBERS = 16
PARTICLES = 16 * MEMBERS
OWNERS = 32
TABLE_ROWS = 8 * OWNERS
PAIR = 2 * NA
IMG_W = SHELLS * PAIR
CTF_W = SHELLS * NA
REF_W = 640
ROW_W = IMG_W + CTF_W
SEND_W = 896
LOGIT_W = 384
FREQS = NA // 2 + 1
TOPPAD = 112
TABLE = 384
UNROLL = 4
CLS = ("x", "zh", "zl")
GROUP = ("zl", "img")
DEVICES = ("x", "zh", "zl", "img")

bf16 = jnp.bfloat16
f32 = jnp.float32


def split3(x):
    x = np.asarray(x, np.float32)
    hi = x.astype(bf16)
    rest = x - hi.astype(np.float32)
    mid = rest.astype(bf16)
    low = (rest - mid.astype(np.float32)).astype(bf16)
    return np.stack([hi, mid, low])


def make_tables():
    freq = np.arange(FREQS)
    angle = np.arange(NA)
    phase = (freq[None, :] * angle[:, None]) % NA * (2.0 * np.pi / NA)
    cos, sin = np.cos(phase), np.sin(phase)
    forward = np.zeros((TABLE, 2 * LANES))
    for part in range(2):
        rows = slice(TOPPAD + part * NA, TOPPAD + part * NA + NA)
        re = slice(part * HALF, part * HALF + FREQS)
        im = slice(LANES + part * HALF, LANES + part * HALF + FREQS)
        forward[rows, re], forward[rows, im] = cos, -sin
    lane = np.arange(SEND_W)
    source = np.where(lane < IMG_W, IMG_W + NA * (lane // PAIR) + lane % NA, lane) - 512
    spread = (np.arange(384)[:, None] == source[None, :]) & (lane < ROW_W)[None, :]
    return split3(forward), spread.astype(bf16)


def dot(a, b):
    return lax.dot_general(a, b, (((1,), (0,)), ((), ())), preferred_element_type=f32)


def dot_t(a, b):
    return lax.dot_general(a, b, (((1,), (1,)), ((), ())), preferred_element_type=f32)


def dot_exact(a, b):
    return lax.dot_general(
        a,
        b,
        (((1,), (0,)), ((), ())),
        precision=lax.Precision.HIGHEST,
        preferred_element_type=f32,
    )


def window(table, block, index):
    start = TOPPAD - 16 * index
    return table[block, start : start + 2 * LANES, :]


def lanes_of(x, index):
    return x[:, LANES * index : LANES * index + 2 * LANES]


def lane_index(shape):
    return lax.broadcasted_iota(jnp.int32, shape, len(shape) - 1)


def inverse_weights():
    freq = lane_index((1, LANES)) % HALF
    ends = (freq == 0) | (freq == NA // 2)
    return jnp.where(freq < FREQS, jnp.where(ends, 1.0 / NA, 2.0 / NA), 0.0).astype(f32)


def put(hat, count, s, y):
    hat[pl.ds(s, count, stride=PITCH), :] = y[:, :LANES]
    hat[pl.ds(8 + s, count, stride=PITCH), :] = y[:, LANES:]


def clear_rest(hat, count):
    zero = jnp.zeros((count, LANES), f32)
    for s in range(WINDOWS, 8):
        hat[pl.ds(s, count, stride=PITCH), :] = zero
        hat[pl.ds(8 + s, count, stride=PITCH), :] = zero


def rows_summed(tiles):
    line = lax.broadcasted_iota(jnp.int32, (8, LANES), 0)
    for k in (1, 2, 4):
        mine = (line & k) == 0
        tiles = [
            jnp.where(mine, a, b) + pltpu.roll(jnp.where(mine, b, a), 8 - k, 0)
            for a, b in zip(tiles[::2], tiles[1::2])
        ]
    return tiles[0]


def forward_wave(x, table, index, splits=3):
    return sum(dot(x, window(table, k, index)) for k in range(splits))


def pack_kernel(images, ctf, classes, place, wsend):
    width = SEND_W - ROW_W
    lookup = place[...].astype(f32).astype(bf16)
    line = lax.broadcasted_iota(jnp.int32, (16, 16), 0)
    listed = jnp.zeros((16, 16), f32)
    for j in range(TOP):
        hit = classes[j : j + 1, :] == lax.broadcasted_iota(jnp.int32, (place.shape[1], 16), 0)
        row = dot(lookup, jnp.where(hit, 1.0, 0.0).astype(bf16))
        listed = jnp.where(line == j, row, listed)
    tail = jnp.concatenate([listed, jnp.zeros((16, width - 16), f32)], axis=1).astype(bf16)
    for h in range(2):
        for i in range(8):
            shell = i * 8 + h * SHELLS
            wsend[h * 8 + i] = jnp.concatenate(
                [
                    images[:, shell * PAIR : shell * PAIR + IMG_W],
                    ctf[:, shell * NA : shell * NA + CTF_W],
                    tail,
                ],
                axis=1,
            )


def copies_kernel(at, refs, rsend):
    start = pl.multiple_of(at[0] * 2 * IMG_W, LANES)
    mine = refs[:, pl.ds(start, 2 * IMG_W)].astype(f32)
    for h in range(2):
        half = mine[:, h * IMG_W : (h + 1) * IMG_W]
        half = jnp.concatenate([half, jnp.zeros((7, REF_W - IMG_W), f32)], axis=1)
        half = jnp.concatenate([half, jnp.zeros((1, REF_W), f32)], axis=0).astype(bf16)
        for o in range(OWNERS):
            if o % 2 == h:
                rsend[o] = half


def weigh_kernel(recv, inv, spread, table, hat):
    scale = dot(recv[:, 512:], spread[...]).reshape(PARTICLES // 8, 8, SEND_W) * inv[...][None]
    scale = scale.reshape(PARTICLES, SEND_W)
    weighted = (recv[...].astype(f32) * scale).astype(bf16)
    for s in range(WINDOWS):
        y = forward_wave(lanes_of(weighted, s), table, s)
        put(hat, PARTICLES, s, y)
    clear_rest(hat, PARTICLES)


def score_kernel(places, recv, table, what, out, rhat, pq, idx, sem):
    copy = pltpu.make_async_copy(places, idx, sem)
    copy.start()
    raw32 = recv[...].astype(f32).reshape(TABLE_ROWS, REF_W)
    raw = raw32.astype(bf16)
    square = raw32 * raw32
    left = square + jnp.concatenate([square[:, NA:], square[:, :NA]], axis=1)
    right = square + jnp.concatenate([square[:, REF_W - NA :], square[:, : REF_W - NA]], axis=1)
    lane = lane_index((1, REF_W))
    even = (lane < NA) | ((lane >= 2 * PAIR) & (lane < 2 * PAIR + NA))
    odd = ((lane >= PAIR + NA) & (lane < 2 * PAIR)) | (
        (lane >= 3 * PAIR + NA) & (lane < 4 * PAIR)
    )
    power = jnp.where(even, left, jnp.where(odd, right, 0.0)).astype(bf16).astype(f32)
    power = (-0.5 * power).astype(bf16)
    for s in range(SHELLS):
        put(rhat, TABLE_ROWS, s, forward_wave(lanes_of(raw, s), table, s))
    for j in range(SHELLS // 2):
        y = sum(forward_wave(lanes_of(power, s), table, s) for s in (2 * j, 2 * j + 1))
        put(rhat, TABLE_ROWS, SHELLS + j, y)
    clear_rest(rhat, TABLE_ROWS)

    def block(b, carry):
        first = b // 2 * 64 + b % 2 * 8
        lines = pl.ds(pl.multiple_of(b * 8, 8), 8)
        rows = []
        for u in range(8):
            at = pl.multiple_of((b * 8 + u) * PITCH, PITCH)
            rows.append((what[pl.ds(at, 8), :], what[pl.ds(at + 8, 8), :]))
        for j in range(TOP):
            p, q = [], []
            for u, (a_re, a_im) in enumerate(rows):
                t = pl.multiple_of(idx[first + (j * 16 + u)], PITCH)
                b_re = rhat[pl.ds(t, 8), :]
                b_im = rhat[pl.ds(t + 8, 8), :]
                p.append(a_re * b_re + a_im * b_im)
                q.append(a_im * b_re - a_re * b_im)
            pq[j, lines, :LANES] = rows_summed(p)
            pq[j, lines, LANES:] = rows_summed(q)
        return carry

    copy.wait()
    lax.fori_loop(0, PARTICLES // 8, block, 0, unroll=UNROLL)
    weights = inverse_weights()
    low = lane_index((1, LANES)) < HALF
    windows = []
    for j in range(0, TOP, 2):
        sides = []
        for at in (0, LANES):
            first, second = pq[j, :, at : at + LANES], pq[j + 1, :, at : at + LANES]
            first = first + pltpu.roll(first, HALF, 1)
            second = second + pltpu.roll(second, HALF, 1)
            sides.append(jnp.where(low, first, second) * weights)
        x = jnp.concatenate(sides, axis=1)
        hi = x.astype(bf16)
        rest = x - hi.astype(f32)
        mid = rest.astype(bf16)
        small = (rest - mid.astype(f32)).astype(bf16)
        t = [window(table, k, j // 2) for k in range(3)]
        y = dot_t(small, t[0]) + dot_t(hi, t[2]) + dot_t(mid, t[1])
        y = y + (dot_t(mid, t[0]) + dot_t(hi, t[1]))
        windows.append(y + dot_t(hi, t[0]))
    out[:, :LANES] = windows[0][:, :LANES]
    out[:, LANES : 2 * LANES] = windows[0][:, LANES:] + windows[1][:, :LANES]
    out[:, 2 * LANES :] = windows[1][:, LANES:]


def softmax_kernel(parts, out):
    logits = parts[0]
    for k in range(1, MEMBERS):
        logits += parts[k]
    logits = jnp.where(lane_index(logits.shape) < TOP * NA, logits, -jnp.inf)
    highest = jnp.max(logits, axis=1, keepdims=True)
    e = jnp.exp(logits - highest)
    posterior = (e / jnp.sum(e, axis=1, keepdims=True)).astype(bf16)
    for k in range(MEMBERS):
        out[k] = posterior


def gather_kernel(places, post, table, what, out, waves, total, idx, sem):
    copy = pltpu.make_async_copy(places, idx, sem)
    copy.start()
    lane = lane_index((1, 2 * LANES))
    for j in range(TOP):
        first = 16 * (j // 2) + NA * (j % 2)
        mine = (lane >= first) & (lane < first + NA)
        x = jnp.where(mine, lanes_of(post[...].astype(f32), j // 2), 0.0).astype(bf16)
        y = forward_wave(x, table, j // 2, splits=2)
        waves[2 * j] = y[:, :LANES] + pltpu.roll(y[:, :LANES], HALF, 1)
        waves[2 * j + 1] = y[:, LANES:] + pltpu.roll(y[:, LANES:], HALF, 1)
    total[...] = jnp.zeros_like(total)

    def block(b, carry):
        first = b // 2 * 64 + b % 2 * 8
        lines = pl.ds(pl.multiple_of(b * 8, 8), 8)
        tiles = [waves[k, lines, :] for k in range(2 * TOP)]
        for u in range(8):
            at = pl.multiple_of((b * 8 + u) * PITCH, PITCH)
            a_re = what[pl.ds(at, 8), :]
            a_im = what[pl.ds(at + 8, 8), :]
            pending = []
            for j in range(TOP):
                t = pl.multiple_of(idx[first + (j * 16 + u)], PITCH)
                g_re = tiles[2 * j][u : u + 1]
                g_im = tiles[2 * j + 1][u : u + 1]
                re = total[pl.ds(t, 8), :] + (a_re * g_re + a_im * g_im)
                im = total[pl.ds(t + 8, 8), :] + (a_im * g_re - a_re * g_im)
                pending.append((t, re, im))
            for t, re, im in pending:
                total[pl.ds(t, 8), :] = re
                total[pl.ds(t + 8, 8), :] = im
        return carry

    copy.wait()
    lax.fori_loop(0, PARTICLES // 8, block, 0)
    weights = inverse_weights()
    before = None
    for s in range(WINDOWS):
        x = jnp.concatenate(
            [total[pl.ds(8 * k + s, TABLE_ROWS, stride=PITCH), :] * weights for k in range(2)],
            axis=1,
        )
        hi = x.astype(bf16)
        low = (x - hi.astype(f32)).astype(bf16)
        t_hi, t_low = window(table, 0, s), window(table, 1, s)
        y = dot_t(hi, t_hi) + dot_t(low, t_hi) + dot_t(hi, t_low)
        tile = y[:, :LANES] if before is None else before + y[:, :LANES]
        out[:, :, LANES * s : LANES * s + LANES] = tile.reshape(OWNERS, 8, LANES).astype(bf16)
        before = y[:, LANES:]
    out[:, :, LANES * WINDOWS :] = before.reshape(OWNERS, 8, LANES).astype(bf16)


def final_kernel(parts, spread, out):
    sums = []
    for h in range(2):
        members = [s for s in range(OWNERS) if s % 2 == h]
        total = parts[members[0]].astype(f32)
        for s in members[1:]:
            total += parts[s].astype(f32)
        sums.append(total)
    total = jnp.concatenate(sums, axis=0)
    under = dot_exact(total[:, 512:] + 1.0, spread[:, :REF_W].astype(f32))[:, :IMG_W]
    new = total[:, :IMG_W] / under
    out[:, :IMG_W] = new[:7]
    out[:, IMG_W:] = new[8:15]


VM = pl.BlockSpec(memory_space=pltpu.VMEM)
SM = pl.BlockSpec(memory_space=pltpu.SMEM)
ANY = pl.BlockSpec(memory_space=pl.ANY)


def call(kernel, name, out_shape, in_specs, args, scratch=(), limit=24):
    out_specs = tuple(VM for _ in out_shape) if isinstance(out_shape, tuple) else VM
    return pl.pallas_call(
        kernel,
        out_shape=out_shape,
        in_specs=in_specs,
        out_specs=out_specs,
        scratch_shapes=scratch,
        compiler_params=pltpu.CompilerParams(vmem_limit_bytes=limit * 1024 * 1024),
        name=name,
    )(*args)


def on_device(images, ctf, classes, class_place, references, sigma2):
    table, spread = make_tables()
    img, h = lax.axis_index("img"), lax.axis_index("zl")
    shape = jax.ShapeDtypeStruct
    wsend = call(
        pack_kernel,
        "pack",
        shape((MEMBERS, 16, SEND_W), bf16),
        [VM] * 4,
        (images, ctf, classes.T, class_place.reshape(1, -1)),
        limit=58,
    )
    rsend = call(
        copies_kernel,
        "copies",
        shape((OWNERS, 8, REF_W), bf16),
        [SM, VM],
        (img.reshape(1), references),
        limit=8,
    )
    wrecv = lax.all_to_all(wsend, GROUP, 0, 0, tiled=True)
    rrecv = lax.all_to_all(rsend, CLS, 0, 0, tiled=True)
    listed = wrecv[:, :TOP, ROW_W : ROW_W + 16].astype(jnp.int32)
    idx = ((listed // 7 * 8 + listed % 7) * PITCH).reshape(-1)
    wrecv = wrecv.reshape(PARTICLES, SEND_W)
    inv = 1.0 / lax.dynamic_slice(sigma2, (img * 8 + h * SHELLS,), (SHELLS,))
    inv = jnp.concatenate(
        [jnp.repeat(inv, PAIR), jnp.repeat(inv, NA), jnp.zeros((SEND_W - ROW_W,), f32)]
    )
    inv = jnp.broadcast_to(inv[None], (8, SEND_W))
    hat = shape((PARTICLES * PITCH, LANES), f32)
    what = call(
        weigh_kernel, "weigh", hat, [VM] * 4, (wrecv, inv, spread, table)
    )
    rows = pltpu.VMEM((TABLE_ROWS * PITCH, LANES), f32)
    places = [pltpu.SMEM((PARTICLES * TOP,), jnp.int32), pltpu.SemaphoreType.DMA]
    partial = call(
        score_kernel,
        "score",
        shape((PARTICLES, LOGIT_W), f32),
        [ANY] + [VM] * 3,
        (idx, rrecv, table, what),
        [rows, pltpu.VMEM((TOP, PARTICLES, 2 * LANES), f32), *places],
    )
    parts = lax.all_to_all(partial.reshape(MEMBERS, 16, LOGIT_W), GROUP, 0, 0, tiled=True)
    post = call(
        softmax_kernel, "softmax", shape((MEMBERS, 16, LOGIT_W), bf16), [VM], (parts,)
    )
    post = lax.all_to_all(post, GROUP, 0, 0, tiled=True).reshape(PARTICLES, LOGIT_W)
    waves = pltpu.VMEM((2 * TOP, PARTICLES, LANES), f32)
    sums = call(
        gather_kernel,
        "gather",
        shape((OWNERS, 8, SEND_W), bf16),
        [ANY] + [VM] * 3,
        (idx, post, table, what),
        [waves, rows, *places],
    )
    arrived = lax.all_to_all(sums, CLS, 0, 0, tiled=True)
    return call(
        final_kernel, "final", shape((7, 2 * IMG_W), f32), [VM, VM], (arrived, spread)
    )


def solution(mesh):
    finer = Mesh(mesh.devices.reshape(4, 4, 2, 8), DEVICES)
    in_specs = (
        P(DEVICES, None),
        P(DEVICES, None),
        P(DEVICES, None),
        P(),
        P(CLS, None),
        P(),
    )
    return jax.shard_map(
        on_device, mesh=finer, in_specs=in_specs, out_specs=P(CLS, "img"), check_vma=False
    )
```

```python
import jax
import jax.numpy as jnp
import numpy as np
from jax import lax
from jax.experimental import pallas as pl
from jax.experimental.pallas import tpu as pltpu
from jax.sharding import Mesh
from jax.sharding import PartitionSpec as P

TOP = 4
NA = 72
HALF = 64
LANES = 128
PITCH = 16
SHELLS = 4
WINDOWS = 6
MEMBERS = 16
PARTICLES = 16 * MEMBERS
OWNERS = 32
TABLE_ROWS = 8 * OWNERS
PAIR = 2 * NA
IMG_W = SHELLS * PAIR
CTF_W = SHELLS * NA
REF_W = 640
ROW_W = IMG_W + CTF_W
SEND_W = 896
LOGIT_W = 384
FREQS = NA // 2 + 1
TOPPAD = 112
TABLE = 384
UNROLL = 2
CLS = ("x", "zh", "zl")
GROUP = ("zl", "img")
DEVICES = ("x", "zh", "zl", "img")

bf16 = jnp.bfloat16
f32 = jnp.float32


def split3(x):
    x = np.asarray(x, np.float32)
    hi = x.astype(bf16)
    rest = x - hi.astype(np.float32)
    mid = rest.astype(bf16)
    low = (rest - mid.astype(np.float32)).astype(bf16)
    return np.stack([hi, mid, low])


def make_tables():
    freq = np.arange(FREQS)
    angle = np.arange(NA)
    phase = (freq[None, :] * angle[:, None]) % NA * (2.0 * np.pi / NA)
    cos, sin = np.cos(phase), np.sin(phase)
    forward = np.zeros((TABLE, 2 * LANES))
    for part in range(2):
        rows = slice(TOPPAD + part * NA, TOPPAD + part * NA + NA)
        re = slice(part * HALF, part * HALF + FREQS)
        im = slice(LANES + part * HALF, LANES + part * HALF + FREQS)
        forward[rows, re], forward[rows, im] = cos, -sin
    lane = np.arange(SEND_W)
    source = np.where(lane < IMG_W, IMG_W + NA * (lane // PAIR) + lane % NA, lane) - 512
    spread = (np.arange(384)[:, None] == source[None, :]) & (lane < ROW_W)[None, :]
    return split3(forward), spread.astype(bf16)


def dot(a, b):
    return lax.dot_general(a, b, (((1,), (0,)), ((), ())), preferred_element_type=f32)


def dot_t(a, b):
    return lax.dot_general(a, b, (((1,), (1,)), ((), ())), preferred_element_type=f32)


def dot_exact(a, b):
    return lax.dot_general(
        a,
        b,
        (((1,), (0,)), ((), ())),
        precision=lax.Precision.HIGHEST,
        preferred_element_type=f32,
    )


def window(table, block, index):
    start = TOPPAD - 16 * index
    return table[block, start : start + 2 * LANES, :]


def lanes_of(x, index):
    return x[:, LANES * index : LANES * index + 2 * LANES]


def lane_index(shape):
    return lax.broadcasted_iota(jnp.int32, shape, len(shape) - 1)


def inverse_weights():
    freq = lane_index((1, LANES)) % HALF
    ends = (freq == 0) | (freq == NA // 2)
    return jnp.where(freq < FREQS, jnp.where(ends, 1.0 / NA, 2.0 / NA), 0.0).astype(f32)


def put(hat, count, s, y):
    hat[pl.ds(s, count, stride=PITCH), :] = y[:, :LANES]
    hat[pl.ds(8 + s, count, stride=PITCH), :] = y[:, LANES:]


def clear_rest(hat, count):
    zero = jnp.zeros((count, LANES), f32)
    for s in range(WINDOWS, 8):
        hat[pl.ds(s, count, stride=PITCH), :] = zero
        hat[pl.ds(8 + s, count, stride=PITCH), :] = zero


def rows_summed(tiles):
    line = lax.broadcasted_iota(jnp.int32, (8, LANES), 0)
    for k in (1, 2, 4):
        mine = (line & k) == 0
        tiles = [
            jnp.where(mine, a, b) + pltpu.roll(jnp.where(mine, b, a), 8 - k, 0)
            for a, b in zip(tiles[::2], tiles[1::2])
        ]
    return tiles[0]


def forward_wave(x, table, index, splits=3):
    return sum(dot(x, window(table, k, index)) for k in range(splits))


def pack_kernel(images, ctf, classes, place, wsend):
    width = SEND_W - ROW_W
    lookup = place[...].astype(f32).astype(bf16)
    line = lax.broadcasted_iota(jnp.int32, (16, 16), 0)
    listed = jnp.zeros((16, 16), f32)
    for j in range(TOP):
        hit = classes[j : j + 1, :] == lax.broadcasted_iota(jnp.int32, (place.shape[1], 16), 0)
        row = dot(lookup, jnp.where(hit, 1.0, 0.0).astype(bf16))
        listed = jnp.where(line == j, row, listed)
    tail = jnp.concatenate([listed, jnp.zeros((16, width - 16), f32)], axis=1).astype(bf16)
    for h in range(2):
        for i in range(8):
            shell = i * 8 + h * SHELLS
            wsend[h * 8 + i] = jnp.concatenate(
                [
                    images[:, shell * PAIR : shell * PAIR + IMG_W],
                    ctf[:, shell * NA : shell * NA + CTF_W],
                    tail,
                ],
                axis=1,
            )


def copies_kernel(at, refs, rsend):
    start = pl.multiple_of(at[0] * 2 * IMG_W, LANES)
    mine = refs[:, pl.ds(start, 2 * IMG_W)].astype(f32)
    for h in range(2):
        half = mine[:, h * IMG_W : (h + 1) * IMG_W]
        half = jnp.concatenate([half, jnp.zeros((7, REF_W - IMG_W), f32)], axis=1)
        half = jnp.concatenate([half, jnp.zeros((1, REF_W), f32)], axis=0).astype(bf16)
        for o in range(OWNERS):
            if o % 2 == h:
                rsend[o] = half


def weigh_kernel(recv, inv, spread, table, hat):
    scale = dot(recv[:, 512:], spread[...]).reshape(PARTICLES // 8, 8, SEND_W) * inv[...][None]
    scale = scale.reshape(PARTICLES, SEND_W)
    weighted = (recv[...].astype(f32) * scale).astype(bf16)
    for s in range(WINDOWS):
        y = forward_wave(lanes_of(weighted, s), table, s)
        put(hat, PARTICLES, s, y)
    clear_rest(hat, PARTICLES)


def score_kernel(places, recv, table, what, out, rhat, pq, idx, sem):
    copy = pltpu.make_async_copy(places, idx, sem)
    copy.start()
    raw32 = recv[...].astype(f32).reshape(TABLE_ROWS, REF_W)
    raw = raw32.astype(bf16)
    square = raw32 * raw32
    left = square + jnp.concatenate([square[:, NA:], square[:, :NA]], axis=1)
    right = square + jnp.concatenate([square[:, REF_W - NA :], square[:, : REF_W - NA]], axis=1)
    lane = lane_index((1, REF_W))
    even = (lane < NA) | ((lane >= 2 * PAIR) & (lane < 2 * PAIR + NA))
    odd = ((lane >= PAIR + NA) & (lane < 2 * PAIR)) | (
        (lane >= 3 * PAIR + NA) & (lane < 4 * PAIR)
    )
    power = jnp.where(even, left, jnp.where(odd, right, 0.0)).astype(bf16).astype(f32)
    power = (-0.5 * power).astype(bf16)
    for s in range(SHELLS):
        put(rhat, TABLE_ROWS, s, forward_wave(lanes_of(raw, s), table, s))
    for j in range(SHELLS // 2):
        y = sum(forward_wave(lanes_of(power, s), table, s) for s in (2 * j, 2 * j + 1))
        put(rhat, TABLE_ROWS, SHELLS + j, y)
    clear_rest(rhat, TABLE_ROWS)

    def block(b, carry):
        first = b // 2 * 64 + b % 2 * 8
        lines = pl.ds(pl.multiple_of(b * 8, 8), 8)
        rows = []
        for u in range(8):
            at = pl.multiple_of((b * 8 + u) * PITCH, PITCH)
            rows.append((what[pl.ds(at, 8), :], what[pl.ds(at + 8, 8), :]))
        for j in range(TOP):
            p, q = [], []
            for u, (a_re, a_im) in enumerate(rows):
                t = pl.multiple_of(idx[first + (j * 16 + u)], PITCH)
                b_re = rhat[pl.ds(t, 8), :]
                b_im = rhat[pl.ds(t + 8, 8), :]
                p.append(a_re * b_re + a_im * b_im)
                q.append(a_im * b_re - a_re * b_im)
            pq[j, lines, :LANES] = rows_summed(p)
            pq[j, lines, LANES:] = rows_summed(q)
        return carry

    copy.wait()
    lax.fori_loop(0, PARTICLES // 8, block, 0, unroll=UNROLL)
    weights = inverse_weights()
    low = lane_index((1, LANES)) < HALF
    windows = []
    for j in range(0, TOP, 2):
        sides = []
        for at in (0, LANES):
            first, second = pq[j, :, at : at + LANES], pq[j + 1, :, at : at + LANES]
            first = first + pltpu.roll(first, HALF, 1)
            second = second + pltpu.roll(second, HALF, 1)
            sides.append(jnp.where(low, first, second) * weights)
        x = jnp.concatenate(sides, axis=1)
        hi = x.astype(bf16)
        rest = x - hi.astype(f32)
        mid = rest.astype(bf16)
        small = (rest - mid.astype(f32)).astype(bf16)
        t = [window(table, k, j // 2) for k in range(3)]
        y = dot_t(small, t[0]) + dot_t(hi, t[2]) + dot_t(mid, t[1])
        y = y + (dot_t(mid, t[0]) + dot_t(hi, t[1]))
        windows.append(y + dot_t(hi, t[0]))
    out[:, :LANES] = windows[0][:, :LANES]
    out[:, LANES : 2 * LANES] = windows[0][:, LANES:] + windows[1][:, :LANES]
    out[:, 2 * LANES :] = windows[1][:, LANES:]


def softmax_kernel(parts, out):
    logits = parts[0]
    for k in range(1, MEMBERS):
        logits += parts[k]
    logits = jnp.where(lane_index(logits.shape) < TOP * NA, logits, -jnp.inf)
    highest = jnp.max(logits, axis=1, keepdims=True)
    e = jnp.exp(logits - highest)
    posterior = (e / jnp.sum(e, axis=1, keepdims=True)).astype(bf16)
    for k in range(MEMBERS):
        out[k] = posterior


def gather_kernel(places, post, table, what, out, waves, total, idx, sem):
    copy = pltpu.make_async_copy(places, idx, sem)
    copy.start()
    lane = lane_index((1, 2 * LANES))
    for j in range(TOP):
        first = 16 * (j // 2) + NA * (j % 2)
        mine = (lane >= first) & (lane < first + NA)
        x = jnp.where(mine, lanes_of(post[...].astype(f32), j // 2), 0.0).astype(bf16)
        y = forward_wave(x, table, j // 2, splits=2)
        waves[2 * j] = y[:, :LANES] + pltpu.roll(y[:, :LANES], HALF, 1)
        waves[2 * j + 1] = y[:, LANES:] + pltpu.roll(y[:, LANES:], HALF, 1)
    total[...] = jnp.zeros_like(total)

    def block(b, carry):
        first = b // 2 * 64 + b % 2 * 8
        lines = pl.ds(pl.multiple_of(b * 8, 8), 8)
        tiles = [waves[k, lines, :] for k in range(2 * TOP)]
        for u in range(8):
            at = pl.multiple_of((b * 8 + u) * PITCH, PITCH)
            a_re = what[pl.ds(at, 8), :]
            a_im = what[pl.ds(at + 8, 8), :]
            pending = []
            for j in range(TOP):
                t = pl.multiple_of(idx[first + (j * 16 + u)], PITCH)
                g_re = tiles[2 * j][u : u + 1]
                g_im = tiles[2 * j + 1][u : u + 1]
                re = total[pl.ds(t, 8), :] + (a_re * g_re + a_im * g_im)
                im = total[pl.ds(t + 8, 8), :] + (a_im * g_re - a_re * g_im)
                pending.append((t, re, im))
            for t, re, im in pending:
                total[pl.ds(t, 8), :] = re
                total[pl.ds(t + 8, 8), :] = im
        return carry

    copy.wait()
    lax.fori_loop(0, PARTICLES // 8, block, 0)
    weights = inverse_weights()
    before = None
    for s in range(WINDOWS):
        x = jnp.concatenate(
            [total[pl.ds(8 * k + s, TABLE_ROWS, stride=PITCH), :] * weights for k in range(2)],
            axis=1,
        )
        hi = x.astype(bf16)
        low = (x - hi.astype(f32)).astype(bf16)
        t_hi, t_low = window(table, 0, s), window(table, 1, s)
        y = dot_t(hi, t_hi) + dot_t(low, t_hi) + dot_t(hi, t_low)
        tile = y[:, :LANES] if before is None else before + y[:, :LANES]
        out[:, :, LANES * s : LANES * s + LANES] = tile.reshape(OWNERS, 8, LANES).astype(bf16)
        before = y[:, LANES:]
    out[:, :, LANES * WINDOWS :] = before.reshape(OWNERS, 8, LANES).astype(bf16)


def final_kernel(parts, spread, out):
    sums = []
    for h in range(2):
        members = [s for s in range(OWNERS) if s % 2 == h]
        total = parts[members[0]].astype(f32)
        for s in members[1:]:
            total += parts[s].astype(f32)
        sums.append(total)
    total = jnp.concatenate(sums, axis=0)
    under = dot_exact(total[:, 512:] + 1.0, spread[:, :REF_W].astype(f32))[:, :IMG_W]
    new = total[:, :IMG_W] / under
    out[:, :IMG_W] = new[:7]
    out[:, IMG_W:] = new[8:15]


VM = pl.BlockSpec(memory_space=pltpu.VMEM)
SM = pl.BlockSpec(memory_space=pltpu.SMEM)
ANY = pl.BlockSpec(memory_space=pl.ANY)


def call(kernel, name, out_shape, in_specs, args, scratch=(), limit=24):
    out_specs = tuple(VM for _ in out_shape) if isinstance(out_shape, tuple) else VM
    return pl.pallas_call(
        kernel,
        out_shape=out_shape,
        in_specs=in_specs,
        out_specs=out_specs,
        scratch_shapes=scratch,
        compiler_params=pltpu.CompilerParams(vmem_limit_bytes=limit * 1024 * 1024),
        name=name,
    )(*args)


def on_device(images, ctf, classes, class_place, references, sigma2):
    table, spread = make_tables()
    img, h = lax.axis_index("img"), lax.axis_index("zl")
    shape = jax.ShapeDtypeStruct
    wsend = call(
        pack_kernel,
        "pack",
        shape((MEMBERS, 16, SEND_W), bf16),
        [VM] * 4,
        (images, ctf, classes.T, class_place.reshape(1, -1)),
        limit=58,
    )
    rsend = call(
        copies_kernel,
        "copies",
        shape((OWNERS, 8, REF_W), bf16),
        [SM, VM],
        (img.reshape(1), references),
        limit=8,
    )
    wrecv = lax.all_to_all(wsend, GROUP, 0, 0, tiled=True)
    rrecv = lax.all_to_all(rsend, CLS, 0, 0, tiled=True)
    listed = wrecv[:, :TOP, ROW_W : ROW_W + 16].astype(jnp.int32)
    idx = ((listed // 7 * 8 + listed % 7) * PITCH).reshape(-1)
    wrecv = wrecv.reshape(PARTICLES, SEND_W)
    inv = 1.0 / lax.dynamic_slice(sigma2, (img * 8 + h * SHELLS,), (SHELLS,))
    inv = jnp.concatenate(
        [jnp.repeat(inv, PAIR), jnp.repeat(inv, NA), jnp.zeros((SEND_W - ROW_W,), f32)]
    )
    inv = jnp.broadcast_to(inv[None], (8, SEND_W))
    hat = shape((PARTICLES * PITCH, LANES), f32)
    what = call(
        weigh_kernel, "weigh", hat, [VM] * 4, (wrecv, inv, spread, table)
    )
    rows = pltpu.VMEM((TABLE_ROWS * PITCH, LANES), f32)
    places = [pltpu.SMEM((PARTICLES * TOP,), jnp.int32), pltpu.SemaphoreType.DMA]
    partial = call(
        score_kernel,
        "score",
        shape((PARTICLES, LOGIT_W), f32),
        [ANY] + [VM] * 3,
        (idx, rrecv, table, what),
        [rows, pltpu.VMEM((TOP, PARTICLES, 2 * LANES), f32), *places],
    )
    parts = lax.all_to_all(partial.reshape(MEMBERS, 16, LOGIT_W), GROUP, 0, 0, tiled=True)
    post = call(
        softmax_kernel, "softmax", shape((MEMBERS, 16, LOGIT_W), bf16), [VM], (parts,)
    )
    post = lax.all_to_all(post, GROUP, 0, 0, tiled=True).reshape(PARTICLES, LOGIT_W)
    waves = pltpu.VMEM((2 * TOP, PARTICLES, LANES), f32)
    sums = call(
        gather_kernel,
        "gather",
        shape((OWNERS, 8, SEND_W), bf16),
        [ANY] + [VM] * 3,
        (idx, post, table, what),
        [waves, rows, *places],
    )
    arrived = lax.all_to_all(sums, CLS, 0, 0, tiled=True)
    return call(
        final_kernel, "final", shape((7, 2 * IMG_W), f32), [VM, VM], (arrived, spread)
    )


def solution(mesh):
    finer = Mesh(mesh.devices.reshape(4, 4, 2, 8), DEVICES)
    in_specs = (
        P(DEVICES, None),
        P(DEVICES, None),
        P(DEVICES, None),
        P(),
        P(CLS, None),
        P(),
    )
    return jax.shard_map(
        on_device, mesh=finer, in_specs=in_specs, out_specs=P(CLS, "img"), check_vma=False
    )
```
